32 devices in a mesh: tm: 16 (over z, y, x), head: 2 (over core).
Axes of the slice: x: 2, y: 2, z: 4, core: 2. Of those that a mesh axis runs over, the one named last changes fastest.
Arguments:
- series: bfloat16 [16, 16384, 512], P(None, 'tm'), may hold values from -6 to 6
- modes: int32 [128], replicated, may hold values from 1 to 8191, as said below
- query_weight: bfloat16 [512, 512], P(None, 'head'), may hold values from -0.25 to 0.25
- mix_weight: float32 [128, 8, 64, 128], P('tm', 'head'), may hold values from -0.5 to 0.5
- out_weight: bfloat16 [512, 512], P(None, 'head'), may hold values from -0.25 to 0.25
Outputs:
- output: bfloat16 [16, 16384, 512], P(None, 'tm', 'head')
The draws below stay inside these ranges and needn't reach their ends.
Inputs may be any that keep to these rules, and one draw needn't show every extreme that they name: `modes`: distinct mode numbers; both 1 and one less than half of 16384 are among them.
All inputs are finite; a program needn't handle non-finite values.
Results may differ from the reference program's by a relative error of at most 0.0075.
Values may be sent and summed in bfloat16 or wider, within the bound.
No kernel may reach another device: no remote copies, remote signals or barrier semaphores. Data moves between devices by JAX's collectives and lax.ppermute only.
A program may use at most 128 MiB of HBM per device.

```python
import math
import jax
import jax.numpy as jnp
from jax import lax

D = 512
H = 8
M = 128
SEQS = 16
E = 64
LENGTH = 16384


def draw_modes(key, part):
    half_length = LENGTH // 2
    inner_modes = jax.random.permutation(key, half_length - 3).astype(jnp.int32) + 2
    chosen = jnp.concatenate([jnp.array([1, half_length - 1], jnp.int32), inner_modes[:M - 2]])
    shuffle = jax.random.permutation(jax.random.fold_in(key, 7), M)
    return chosen[shuffle]


def block_levels(rng, extent, pieces, least, high):
    def one(dim, blocks):
        steps = jax.random.uniform(jax.random.fold_in(jax.random.fold_in(rng, 6), dim), (blocks,), jnp.float32, least / len(pieces), high / len(pieces))
        return jnp.repeat(jnp.exp(steps), extent[dim] // blocks).reshape((-1,) + (1,) * (len(extent) - dim - 1))

    level = one(*pieces[0])
    for cut in pieces[1:]:
        level = level * one(*cut)
    return level


def scatter_about(stream_key, dims, spread, bound, pieces=(), kind=jnp.bfloat16):
    drawn = jax.random.normal(stream_key, dims, jnp.float32) * spread
    if len(pieces) > 0:
        drawn = block_levels(stream_key, dims, pieces, -0.22, 0.18) * drawn
    return jnp.clip(drawn, min=-bound, max=bound).astype(kind)


def setup_inputs(seed: int = 0) -> dict:
    streams_of = jax.random.split(jax.random.key(seed), 6)
    return {
        "series": scatter_about(streams_of[0], (SEQS, LENGTH, D), 1.0, 6.0, ((1, 16),)),
        "modes": draw_modes(jax.random.fold_in(streams_of[5], 71), 0),
        "query_weight": scatter_about(streams_of[2], (D, D), D ** -0.5, 0.25, ((1, 2),)),
        "mix_weight": scatter_about(streams_of[3], (M, H, E, 2 * E), (2 * E) ** -0.5, 0.5, ((0, 16), (1, 2)), jnp.float32),
        "out_weight": scatter_about(streams_of[4], (D, D), D ** -0.5, 0.25, ((1, 2),)),
    }


two_pi = 2.0 * math.pi

def wave_tables(mode_list, first_time, time_count, series_length):
    time_index = first_time + lax.iota(jnp.int32, time_count)
    phases = time_index[:, None] * mode_list[None, :] % series_length
    angles = phases.astype(jnp.float32) * (two_pi / series_length)
    return (jnp.cos(angles).astype(jnp.bfloat16), jnp.sin(angles).astype(jnp.bfloat16))

def reference(series, modes, query_weight, mix_weight, out_weight):
    series_count = series.shape[0]
    block_rows = min(LENGTH, 8192)
    block_total = LENGTH // block_rows
    forward_scale = 1.0 / math.sqrt(LENGTH)
    inverse_scale = 1.0 / math.sqrt(M)
    highest = lax.Precision.HIGHEST
    block_ids = jnp.arange(block_total, dtype=jnp.int32)

    def forward_block(running, block_index):
        first_time = (block_index * block_rows).astype(jnp.int32)
        block_series = lax.dynamic_slice_in_dim(series, first_time, block_rows, 1)
        queries = jnp.dot(block_series.reshape(-1, D), query_weight, preferred_element_type=jnp.float32)
        queries = queries.astype(jnp.bfloat16).reshape(series_count, block_rows, D).astype(jnp.float32)
        cosine, sine_part = wave_tables(modes, first_time, block_rows, LENGTH)
        real_part = jnp.einsum('tm,btf->mbf', cosine.astype(jnp.float32), queries, precision=highest)
        imag_part = jnp.einsum('tm,btf->mbf', sine_part.astype(jnp.float32), queries, precision=highest)
        return (running + jnp.stack([real_part, -imag_part], axis=1) * forward_scale, None)
    spectrum, _ = lax.scan(forward_block, jnp.zeros((M, 2, series_count, D), jnp.float32), block_ids)
    spec_parts = spectrum.reshape(M, 2, series_count, H, E)
    from_real = jnp.einsum('mbhi,mhio->mbho', spec_parts[:, 0], mix_weight, precision=highest)
    from_imag = jnp.einsum('mbhi,mhio->mbho', spec_parts[:, 1], mix_weight, precision=highest)
    mixed_real = from_real[..., :E] - from_imag[..., E:]
    mixed_imag = from_real[..., E:] + from_imag[..., :E]
    mixed_spectra = jnp.stack([mixed_real, mixed_imag], axis=1).reshape(M, 2, series_count, D)
    mixed_spectra = mixed_spectra.astype(jnp.bfloat16).astype(jnp.float32)

    def inverse_block(running, block_index):
        first_time = (block_index * block_rows).astype(jnp.int32)
        cosine, sine_part = wave_tables(modes, first_time, block_rows, LENGTH)
        summed = jnp.einsum('tm,mbf->btf', cosine.astype(jnp.float32), mixed_spectra[:, 0], precision=highest)
        summed = summed - jnp.einsum('tm,mbf->btf', sine_part.astype(jnp.float32), mixed_spectra[:, 1], precision=highest)
        restored = (summed * inverse_scale).astype(jnp.bfloat16)
        output = jnp.dot(restored.reshape(-1, D), out_weight, preferred_element_type=jnp.float32)
        return (running, output.astype(jnp.bfloat16).reshape(series_count, block_rows, D))
    _, stacked = lax.scan(inverse_block, jnp.zeros((), jnp.float32), block_ids)
    return jnp.moveaxis(stacked, 0, 1).reshape(series_count, LENGTH, D)
```

```python
import functools
import math

import jax
import jax.numpy as jnp
from jax import lax
from jax.experimental import pallas as pl
from jax.experimental.pallas import tpu as pltpu
from jax.sharding import PartitionSpec as P

f32 = jnp.float32
bf16 = jnp.bfloat16
two_pi = 2.0 * math.pi


def row_modes(place, modes_row, rows, own_modes, series_length):
    lanes = modes_row.shape[1]
    row = lax.broadcasted_iota(jnp.int32, (rows, lanes), 0)
    lane = lax.broadcasted_iota(jnp.int32, (rows, lanes), 1)
    block_rows = 2 * own_modes
    far = rows // block_rows // 4
    block = row // block_rows
    inside = row - block * block_rows
    quarter = block // far
    relative = (quarter // 2) + 2 * (quarter % 2) + 4 * (block % far)
    imaginary = inside // own_modes
    wanted = (place ^ relative) * own_modes + inside - imaginary * own_modes
    picked = jnp.where(lane == wanted, modes_row.astype(f32), 0.0)
    mode = jnp.sum(picked, axis=1, keepdims=True).astype(jnp.int32)
    return mode, imaginary[:, :1] * (series_length // 4)


def wave(phases, series_length):
    turns = phases.astype(f32) * (1.0 / series_length)
    quarters = jnp.floor(turns * 4.0 + 0.5)
    angle = (turns - quarters * 0.25) * two_pi
    square = angle * angle
    cosine = 1.0 + square * (-0.5 + square * (1 / 24 + square * (-1 / 720 + square * (1 / 40320))))
    sine = angle * (1.0 + square * (-1 / 6 + square * (1 / 120 + square * (-1 / 5040))))
    which = quarters.astype(jnp.int32)
    size = jnp.where(which & 1 == 0, cosine, sine)
    return jnp.where((which == 1) | (which == 2), -size, size)


def forward_kernel(first, own_modes, series_length, place_ref, *refs):
    if first:
        modes_ref, series_ref, send_ref, keep_ref, table_ref = refs
        rows, time_count = table_ref.shape

        @pl.when(pl.program_id(0) == 0)
        def _():
            place = place_ref[0]
            mode, shift = row_modes(place, modes_ref[...], rows, own_modes, series_length)
            step = 16
            for start in range(0, rows, step):
                time_index = place * time_count + lax.broadcasted_iota(jnp.int32, (step, time_count), 1)
                phases = time_index * mode[start:start + step] + shift[start:start + step]
                phases = phases & (series_length - 1)
                table_ref[start:start + step, :] = wave(phases, series_length).astype(bf16)
    else:
        table_ref, series_ref, send_ref, keep_ref = refs
    part = jnp.dot(table_ref[...], series_ref[0], preferred_element_type=f32)
    q = part.shape[0] // 4
    if first:
        send_ref[0] = part[2 * q:].astype(bf16)
        keep_ref[0] = part[:2 * q]
    else:
        send_ref[0, :q] = part[q:2 * q].astype(bf16)
        send_ref[0, q:] = part[3 * q:].astype(bf16)
        keep_ref[0, :q] = part[:q]
        keep_ref[0, q:] = part[2 * q:3 * q]


def forward(first, series, place, extra, count, half, own_modes, series_length, rows):
    _, time_count, width = series.shape
    offset = 0 if first else count
    series_spec = pl.BlockSpec((1, time_count, width), lambda b, p: (p[1] * half + offset + b, 0, 0))
    table_spec = pl.BlockSpec((rows, time_count), lambda b, p: (0, 0))
    part_spec = pl.BlockSpec((1, rows // 2, width), lambda b, p: (b, 0, 0))
    outs = [jax.ShapeDtypeStruct((count, rows // 2, width), bf16), jax.ShapeDtypeStruct((count, rows // 2, width), f32)]
    out_specs = [part_spec, part_spec]
    if first:
        in_specs = [pl.BlockSpec(extra.shape, lambda b, p: (0, 0)), series_spec]
        outs.append(jax.ShapeDtypeStruct((rows, time_count), bf16))
        out_specs.append(table_spec)
    else:
        in_specs = [table_spec, series_spec]
    return pl.pallas_call(
        functools.partial(forward_kernel, first, own_modes, series_length),
        out_shape=outs,
        grid_spec=pltpu.PrefetchScalarGridSpec(num_scalar_prefetch=1, grid=(count,), in_specs=in_specs, out_specs=out_specs),
        compiler_params=pltpu.CompilerParams(vmem_limit_bytes=24 * 2**20),
        cost_estimate=pl.CostEstimate(
            flops=2 * count * rows * time_count * width,
            bytes_accessed=count * (time_count * width * 2 + rows * width * 3),
            transcendentals=0,
        ),
        name="forward_first" if first else "forward_second",
    )(place, extra, series)


def split_rows(value):
    high = value.astype(bf16)
    low = (value - high.astype(f32)).astype(bf16)
    return jnp.concatenate([high, low], axis=0)


def fold_rows(value):
    half = value.shape[0] // 2
    return value[:half] + value[half:]


def mix_kernel(scale, own_modes, arrivals, own_ref, *refs):
    arrived = refs[:arrivals]
    query_ref, mix_ref, out_weight_ref, here_ref, there_ref = refs[arrivals:]
    total = own_ref[...]
    for ref in arrived:
        total = total + ref[...].astype(f32)
    total = total * scale
    count, _, width = total.shape
    rows = count * own_modes
    heads = mix_ref.shape[0]
    spectrum = jnp.concatenate(
        [total[:, :own_modes].reshape(rows, width), total[:, own_modes:].reshape(rows, width)], axis=0
    )
    queries = fold_rows(jnp.dot(split_rows(spectrum), query_ref[...], preferred_element_type=f32))
    lower = lax.broadcasted_iota(jnp.int32, (rows, 128), 1) < 64
    row_mode = lax.broadcasted_iota(jnp.int32, (2 * rows, 128), 0) % own_modes
    mixed_real, mixed_imag = [], []
    for pair in range(heads // 2):
        columns = slice(pair * 128, pair * 128 + 128)
        real, imag = queries[:rows, columns], queries[rows:, columns]
        both = [
            jnp.where(lower, real, pltpu.roll(imag, 64, 1)),
            jnp.where(lower, pltpu.roll(real, 64, 1), imag),
        ]
        mixed = []
        for which in range(2):
            pieces = split_rows(both[which])
            zero = jnp.zeros_like(pieces)
            spread = jnp.concatenate([jnp.where(row_mode == k, pieces, zero) for k in range(own_modes)], axis=1)
            mixed.append(fold_rows(jnp.dot(spread, mix_ref[2 * pair + which], preferred_element_type=f32)))
        mixed_real.append(jnp.where(lower, mixed[0], pltpu.roll(mixed[1], 64, 1)))
        mixed_imag.append(jnp.where(lower, pltpu.roll(mixed[0], 64, 1), mixed[1]))
    mixed = jnp.concatenate([jnp.concatenate(mixed_real, axis=1), jnp.concatenate(mixed_imag, axis=1)], axis=0)
    result = fold_rows(jnp.dot(split_rows(mixed), out_weight_ref[...], preferred_element_type=f32)).astype(bf16)
    here = here_ref.shape[2]
    both = jnp.concatenate(
        [result[:rows].reshape(count, own_modes, width), result[rows:].reshape(count, own_modes, width)], axis=1
    )
    here_ref[...] = both[:, :, :here]
    there_ref[...] = both[:, :, here:]


def mix(own, arrived, query_full, mix_full, out_full, scale, own_modes):
    count, block_rows, width = own.shape
    here = width // 2
    heads = mix_full.shape[0]
    if own_modes % 8 == 0:
        shape = jax.ShapeDtypeStruct((count, block_rows, here), bf16)
        return pl.pallas_call(
            functools.partial(mix_kernel, scale, own_modes, len(arrived)),
            out_shape=[shape, shape],
            compiler_params=pltpu.CompilerParams(vmem_limit_bytes=32 * 2**20),
            cost_estimate=pl.CostEstimate(flops=3 * 10**9, bytes_accessed=4 * 2**20, transcendentals=0),
            name="mix_modes",
        )(own, *arrived, query_full, mix_full, out_full)
    total = (own + sum(piece.astype(f32) for piece in arrived)) * scale
    queries = jnp.einsum("brf,fg->brg", total, query_full.astype(f32), precision=lax.Precision.HIGHEST)
    queries = queries.reshape(count, 2, own_modes, heads, 64)
    weights = mix_full.reshape(heads, own_modes, 2, 64, 2, 64).astype(f32)
    mixed = jnp.einsum("brmhi,hmriso->bsmho", queries, weights, precision=lax.Precision.HIGHEST)
    mixed = mixed.reshape(count, block_rows, width)
    result = jnp.einsum("brf,fg->brg", mixed, out_full.astype(f32), precision=lax.Precision.HIGHEST).astype(bf16)
    return result[:, :, :here], result[:, :, here:]


def inverse_kernel(scale, aliased, place_ref, table_ref, *refs):
    pieces, out_ref = refs[:4], refs[-1]
    spectra = jnp.concatenate([piece[0] for piece in pieces], axis=0)
    result = jnp.dot(table_ref[...], spectra, preferred_element_type=f32) * scale
    out_ref[0] = result.astype(bf16)


def inverse(place, table, pieces, previous, series_count, half, offset, scale):
    time_count, rows = table.shape
    count, quarter, width = pieces[0].shape
    own = count // 2
    piece_spec = pl.BlockSpec((1, quarter, width), lambda b, p: (b, 0, 0))
    in_specs = [pl.BlockSpec((time_count, rows), lambda b, p: (0, 0))] + [piece_spec] * 4
    args = [place, table, *pieces]
    aliases = {}
    if previous is not None:
        in_specs.append(pl.BlockSpec(memory_space=pl.ANY))
        aliases = {len(args): 0}
        args.append(previous)
    return pl.pallas_call(
        functools.partial(inverse_kernel, scale, previous is not None),
        out_shape=jax.ShapeDtypeStruct((series_count, time_count, width), bf16),
        grid_spec=pltpu.PrefetchScalarGridSpec(
            num_scalar_prefetch=1,
            grid=(count,),
            in_specs=in_specs,
            out_specs=pl.BlockSpec(
                (1, time_count, width), lambda b, p: ((p[1] ^ (b // own)) * half + offset + b % own, 0, 0)
            ),
        ),
        input_output_aliases=aliases,
        compiler_params=pltpu.CompilerParams(vmem_limit_bytes=24 * 2**20),
        cost_estimate=pl.CostEstimate(
            flops=2 * count * time_count * rows * width,
            bytes_accessed=count * (time_count * width * 2 + rows * width * 2),
            transcendentals=0,
        ),
        name="inverse_second" if previous is not None else "inverse_first",
    )(*args)


def to_device(value, mask, size):
    return lax.ppermute(value, "tm", [(i, i ^ mask) for i in range(size)])


def to_core(value):
    return lax.ppermute(value, "head", [(0, 1), (1, 0)])


def reduce_scatter(send, keep, masks, size, block_rows):
    q = keep.shape[1] // 2
    arrived = to_device(send, masks[0], size)
    onward = (keep[:, q:] + arrived[:, q:].astype(f32)).astype(bf16)
    second = to_device(onward, masks[1], size)
    total = keep[:, :q] + arrived[:, :q].astype(f32) + second.astype(f32)
    pieces = []
    for far in range(1, q // block_rows):
        part = total[:, far * block_rows:(far + 1) * block_rows].astype(bf16)
        pieces.append(to_device(part, 4 * far, size))
    return total[:, :block_rows], pieces


def gather(block, swapped, size):
    far = [block] + [to_device(block, 4 * z, size) for z in range(1, size // 4)]
    own = jnp.concatenate(far, axis=1)
    by_x = to_device(own, 1, size)
    by_y = to_device(own, 2, size)
    by_both = to_device(by_x, 2, size) if swapped else to_device(by_y, 1, size)
    return [own, by_y, by_x, by_both]


def body(series, modes, query_weight, mix_weight, out_weight):
    series_count, shard_rows, width = series.shape
    own_modes, heads_here, head_size, _ = mix_weight.shape
    mode_total = modes.shape[0]
    size = lax.axis_size("tm")
    series_length = size * shard_rows
    rows = 2 * mode_total
    half = series_count // 2
    count = half // 2
    core = lax.axis_index("head")
    place = jnp.stack([lax.axis_index("tm"), core]).astype(jnp.int32)

    send_a, keep_a, table = forward(
        True, series, place, modes[None, :], count, half, own_modes, series_length, rows
    )
    send_b, keep_b = forward(False, series, place, table, count, half, own_modes, series_length, rows)

    real, imag = mix_weight[..., :head_size], mix_weight[..., head_size:]
    mix_here = jnp.concatenate(
        [jnp.concatenate([real, imag], axis=-1), jnp.concatenate([-imag, real], axis=-1)], axis=2
    ).astype(bf16)
    mix_here = jnp.swapaxes(mix_here, 0, 1).reshape(heads_here, own_modes * 2 * head_size, 2 * head_size)
    mix_full = jnp.concatenate([mix_here, to_core(mix_here)], axis=0)
    query_full = jnp.concatenate([query_weight, to_core(query_weight)], axis=1)
    out_full = jnp.concatenate([out_weight, to_core(out_weight)], axis=1)
    out_full = jnp.where(core == 0, out_full, jnp.roll(out_full, width // 2, axis=0))
    table_back = table.T

    block_rows = 2 * own_modes
    scale = 1.0 / math.sqrt(series_length)
    back_scale = 1.0 / math.sqrt(mode_total)
    total_a = reduce_scatter(send_a, keep_a, (1, 2), size, block_rows)
    total_b = reduce_scatter(send_b, keep_b, (2, 1), size, block_rows)
    gathered = []
    for part, (own, arrived) in enumerate((total_a, total_b)):
        here, there = mix(own, arrived, query_full, mix_full, out_full, scale, own_modes)
        block = jnp.concatenate([here, to_core(there)], axis=0)
        gathered.append(gather(block, part == 1, size))
    output = inverse(place, table_back, gathered[0], None, series_count, half, 0, back_scale)
    return inverse(place, table_back, gathered[1], output, series_count, half, count, back_scale)


def solution(mesh):
    in_specs = (
        P(None, "tm", None),
        P(),
        P(None, "head"),
        P("tm", "head", None, None),
        P(None, "head"),
    )
    out_specs = P(None, "tm", "head")
    return jax.shard_map(body, mesh=mesh, in_specs=in_specs, out_specs=out_specs, check_vma=False)
```

```python
import functools
import math

import jax
import jax.numpy as jnp
from jax import lax
from jax.experimental import pallas as pl
from jax.experimental.pallas import tpu as pltpu
from jax.sharding import PartitionSpec as P

f32 = jnp.float32
bf16 = jnp.bfloat16
two_pi = 2.0 * math.pi


def row_modes(place, core, modes_row, rows, own_modes, series_length):
    lanes = modes_row.shape[1]
    row = lax.broadcasted_iota(jnp.int32, (rows, lanes), 0)
    lane = lax.broadcasted_iota(jnp.int32, (rows, lanes), 1)
    block_rows = 2 * own_modes
    far = rows // block_rows // 4
    block = row // block_rows
    inside = row - block * block_rows
    quarter = block // far
    relative = (quarter // 2) * (1 + core) + (quarter % 2) * (2 - core) + 4 * (block % far)
    imaginary = inside // own_modes
    wanted = (place ^ relative) * own_modes + inside - imaginary * own_modes
    picked = jnp.where(lane == wanted, modes_row.astype(f32), 0.0)
    mode = jnp.sum(picked, axis=1, keepdims=True).astype(jnp.int32)
    return mode, imaginary[:, :1] * (series_length // 4)


def wave(phases, series_length):
    turns = phases.astype(f32) * (1.0 / series_length)
    quarters = jnp.floor(turns * 4.0 + 0.5)
    angle = (turns - quarters * 0.25) * two_pi
    square = angle * angle
    cosine = 1.0 + square * (-0.5 + square * (1 / 24 + square * (-1 / 720 + square * (1 / 40320))))
    sine = angle * (1.0 + square * (-1 / 6 + square * (1 / 120 + square * (-1 / 5040))))
    which = quarters.astype(jnp.int32)
    odd = which & 1 == 1
    cos_size = jnp.where(odd, sine, cosine)
    sin_size = jnp.where(odd, cosine, sine)
    cos_flip = (which == 1) | (which == 2)
    sin_flip = (which == 2) | (which == 3)
    return jnp.where(cos_flip, -cos_size, cos_size), jnp.where(sin_flip, -sin_size, sin_size)


def fill_table(place_ref, modes_ref, table_ref, own_modes, series_length):
    rows, time_count = table_ref.shape
    place = place_ref[0]
    mode, shift = row_modes(place, place_ref[1], modes_ref[...], rows, own_modes, series_length)
    lane = lax.broadcasted_iota(jnp.int32, (rows, 128), 1)
    last = series_length - 1
    cos_a, sin_a = wave((mode * (place * time_count + lane * 128) + shift) & last, series_length)
    cos_b, sin_b = wave((mode * lane) & last, series_length)
    for piece in range(time_count // 128):
        value = cos_a[:, piece:piece + 1] * cos_b - sin_a[:, piece:piece + 1] * sin_b
        table_ref[:, piece * 128:piece * 128 + 128] = value.astype(bf16)


def forward_kernel(first, count, half, own_modes, series_length, place_ref, extra_ref, series_ref, *refs):
    if first:
        send_ref, keep_ref, table_ref, held, sems = refs
    else:
        send_ref, keep_ref, held, sems = refs
        table_ref = extra_ref
    base = place_ref[1] * half + (0 if first else count)
    copies = [pltpu.make_async_copy(series_ref.at[base + b], held.at[b], sems.at[b]) for b in range(count)]
    for copy in copies:
        copy.start()
    if first:
        fill_table(place_ref, extra_ref, table_ref, own_modes, series_length)
    middle = table_ref.shape[0] // 2
    for b in range(count):
        copies[b].wait()
        part = jnp.dot(table_ref[...], held[b], preferred_element_type=f32)
        send_ref[b] = part[middle:].astype(bf16)
        keep_ref[b] = part[:middle]


def forward(first, series, place, extra, count, half, own_modes, series_length, rows):
    _, time_count, width = series.shape
    whole = pl.BlockSpec(memory_space=pltpu.VMEM)
    outs = [jax.ShapeDtypeStruct((count, rows // 2, width), bf16), jax.ShapeDtypeStruct((count, rows // 2, width), f32)]
    if first:
        outs.append(jax.ShapeDtypeStruct((rows, time_count), bf16))
    return pl.pallas_call(
        functools.partial(forward_kernel, first, count, half, own_modes, series_length),
        out_shape=outs,
        in_specs=[pl.BlockSpec(memory_space=pltpu.SMEM), whole, pl.BlockSpec(memory_space=pltpu.HBM)],
        out_specs=[whole] * len(outs),
        scratch_shapes=[pltpu.VMEM((count, time_count, width), bf16), pltpu.SemaphoreType.DMA((count,))],
        compiler_params=pltpu.CompilerParams(vmem_limit_bytes=50 * 2**20),
        cost_estimate=pl.CostEstimate(
            flops=2 * count * rows * time_count * width,
            bytes_accessed=count * (time_count * width * 2 + rows * width * 3),
            transcendentals=0,
        ),
        name="forward_first" if first else "forward_second",
    )(place, extra, series)


def split_rows(value):
    high = value.astype(bf16)
    low = (value - high.astype(f32)).astype(bf16)
    return jnp.concatenate([high, low], axis=0)


def fold_rows(value):
    half = value.shape[0] // 2
    return value[:half] + value[half:]


def mix_kernel(scale, own_modes, arrivals, own_ref, *refs):
    arrived = refs[:arrivals]
    query_ref, mix_ref, out_weight_ref, here_ref, there_ref = refs[arrivals:]
    total = own_ref[...]
    for ref in arrived:
        total = total + ref[...].astype(f32)
    total = total * scale
    count, _, width = total.shape
    rows = count * own_modes
    heads = mix_ref.shape[0]
    spectrum = jnp.concatenate(
        [total[:, :own_modes].reshape(rows, width), total[:, own_modes:].reshape(rows, width)], axis=0
    )
    queries = fold_rows(jnp.dot(split_rows(spectrum), query_ref[...], preferred_element_type=f32))
    lower = lax.broadcasted_iota(jnp.int32, (rows, 128), 1) < 64
    row_mode = lax.broadcasted_iota(jnp.int32, (2 * rows, 128), 0) % own_modes
    mixed_real, mixed_imag = [], []
    for pair in range(heads // 2):
        columns = slice(pair * 128, pair * 128 + 128)
        real, imag = queries[:rows, columns], queries[rows:, columns]
        both = [
            jnp.where(lower, real, pltpu.roll(imag, 64, 1)),
            jnp.where(lower, pltpu.roll(real, 64, 1), imag),
        ]
        mixed = []
        for which in range(2):
            pieces = split_rows(both[which])
            zero = jnp.zeros_like(pieces)
            spread = jnp.concatenate([jnp.where(row_mode == k, pieces, zero) for k in range(own_modes)], axis=1)
            mixed.append(fold_rows(jnp.dot(spread, mix_ref[2 * pair + which], preferred_element_type=f32)))
        mixed_real.append(jnp.where(lower, mixed[0], pltpu.roll(mixed[1], 64, 1)))
        mixed_imag.append(jnp.where(lower, pltpu.roll(mixed[0], 64, 1), mixed[1]))
    mixed = jnp.concatenate([jnp.concatenate(mixed_real, axis=1), jnp.concatenate(mixed_imag, axis=1)], axis=0)
    result = fold_rows(jnp.dot(split_rows(mixed), out_weight_ref[...], preferred_element_type=f32)).astype(bf16)
    here = here_ref.shape[2]
    both = jnp.concatenate(
        [result[:rows].reshape(count, own_modes, width), result[rows:].reshape(count, own_modes, width)], axis=1
    )
    here_ref[...] = both[:, :, :here]
    there_ref[...] = both[:, :, here:]


def mix(own, arrived, query_full, mix_full, out_full, scale, own_modes):
    count, block_rows, width = own.shape
    here = width // 2
    heads = mix_full.shape[0]
    if own_modes % 8 == 0:
        shape = jax.ShapeDtypeStruct((count, block_rows, here), bf16)
        return pl.pallas_call(
            functools.partial(mix_kernel, scale, own_modes, len(arrived)),
            out_shape=[shape, shape],
            compiler_params=pltpu.CompilerParams(vmem_limit_bytes=32 * 2**20),
            cost_estimate=pl.CostEstimate(flops=3 * 10**9, bytes_accessed=4 * 2**20, transcendentals=0),
            name="mix_modes",
        )(own, *arrived, query_full, mix_full, out_full)
    total = (own + sum(piece.astype(f32) for piece in arrived)) * scale
    queries = jnp.einsum("brf,fg->brg", total, query_full.astype(f32), precision=lax.Precision.HIGHEST)
    queries = queries.reshape(count, 2, own_modes, heads, 64)
    weights = mix_full.reshape(heads, own_modes, 2, 64, 2, 64).astype(f32)
    mixed = jnp.einsum("brmhi,hmriso->bsmho", queries, weights, precision=lax.Precision.HIGHEST)
    mixed = mixed.reshape(count, block_rows, width)
    result = jnp.einsum("brf,fg->brg", mixed, out_full.astype(f32), precision=lax.Precision.HIGHEST).astype(bf16)
    return result[:, :, :here], result[:, :, here:]


def inverse_kernel(scale, half, offset, place_ref, table_ref, *refs):
    pieces, (out_ref, held, sems) = refs[:4], refs[-3:]
    count = held.shape[0]
    own = count // 2
    copies = []
    for b in range(count):
        spectra = jnp.concatenate([piece[b] for piece in pieces], axis=0)
        result = jnp.dot(table_ref[...], spectra, preferred_element_type=f32) * scale
        held[b] = result.astype(bf16)
        index = (place_ref[1] ^ (b // own)) * half + offset + b % own
        copies.append(pltpu.make_async_copy(held.at[b], out_ref.at[index], sems.at[b]))
        copies[-1].start()
    for copy in copies:
        copy.wait()


def inverse(place, table, pieces, previous, series_count, half, offset, scale):
    time_count, rows = table.shape
    count, _, width = pieces[0].shape
    whole = pl.BlockSpec(memory_space=pltpu.VMEM)
    in_specs = [pl.BlockSpec(memory_space=pltpu.SMEM)] + [whole] * 5
    args = [place, table, *pieces]
    aliases = {}
    if previous is not None:
        in_specs.append(pl.BlockSpec(memory_space=pltpu.HBM))
        aliases = {len(args): 0}
        args.append(previous)
    return pl.pallas_call(
        functools.partial(inverse_kernel, scale, half, offset),
        out_shape=jax.ShapeDtypeStruct((series_count, time_count, width), bf16),
        in_specs=in_specs,
        out_specs=pl.BlockSpec(memory_space=pltpu.HBM),
        scratch_shapes=[pltpu.VMEM((count, time_count, width), bf16), pltpu.SemaphoreType.DMA((count,))],
        input_output_aliases=aliases,
        compiler_params=pltpu.CompilerParams(vmem_limit_bytes=32 * 2**20),
        cost_estimate=pl.CostEstimate(
            flops=2 * count * time_count * rows * width,
            bytes_accessed=count * (time_count * width * 2 + rows * width * 2),
            transcendentals=0,
        ),
        name="inverse_first" if previous is None else "inverse_second",
    )(*args)


def to_devices(value, masks, size):
    pairs = [(2 * i + c, 2 * (i ^ masks[c]) + c) for i in range(size) for c in range(2)]
    return lax.ppermute(value, ("tm", "head"), pairs)


going_first, going_second = (1, 2), (2, 1)


def to_core(value):
    return lax.ppermute(value, "head", [(0, 1), (1, 0)])


def reduce_scatter(send, keep, size, block_rows):
    q = keep.shape[1] // 2
    arrived = to_devices(send, going_first, size)
    onward = (keep[:, q:] + arrived[:, q:].astype(f32)).astype(bf16)
    second = to_devices(onward, going_second, size)
    total = keep[:, :q] + arrived[:, :q].astype(f32) + second.astype(f32)
    pieces = []
    for far in range(1, q // block_rows):
        part = total[:, far * block_rows:(far + 1) * block_rows].astype(bf16)
        pieces.append(to_devices(part, (4 * far, 4 * far), size))
    return total[:, :block_rows], pieces


def gather(block, size):
    far = [block] + [to_devices(block, (4 * z, 4 * z), size) for z in range(1, size // 4)]
    own = jnp.concatenate(far, axis=1)
    by_second = to_devices(own, going_second, size)
    by_first = to_devices(own, going_first, size)
    by_both = to_devices(by_second, going_first, size)
    return [own, by_second, by_first, by_both]


def body(series, modes, query_weight, mix_weight, out_weight):
    series_count, shard_rows, width = series.shape
    own_modes, heads_here, head_size, _ = mix_weight.shape
    mode_total = modes.shape[0]
    size = lax.axis_size("tm")
    series_length = size * shard_rows
    rows = 2 * mode_total
    half = series_count // 2
    count = half // 2
    core = lax.axis_index("head")
    place = jnp.stack([lax.axis_index("tm"), core]).astype(jnp.int32)

    send_a, keep_a, table = forward(
        True, series, place, modes[None, :], count, half, own_modes, series_length, rows
    )
    send_b, keep_b = forward(False, series, place, table, count, half, own_modes, series_length, rows)
    table, query_weight, mix_weight, out_weight = lax.optimization_barrier((table, query_weight, mix_weight, out_weight))

    real, imag = mix_weight[..., :head_size], mix_weight[..., head_size:]
    mix_here = jnp.concatenate(
        [jnp.concatenate([real, imag], axis=-1), jnp.concatenate([-imag, real], axis=-1)], axis=2
    ).astype(bf16)
    mix_here = jnp.swapaxes(mix_here, 0, 1).reshape(heads_here, own_modes * 2 * head_size, 2 * head_size)
    mix_full = jnp.concatenate([mix_here, to_core(mix_here)], axis=0)
    query_full = jnp.concatenate([query_weight, to_core(query_weight)], axis=1)
    out_full = jnp.concatenate([out_weight, to_core(out_weight)], axis=1)
    out_full = jnp.where(core == 0, out_full, jnp.roll(out_full, width // 2, axis=0))
    table_back = table.T

    block_rows = 2 * own_modes
    scale = 1.0 / math.sqrt(series_length)
    back_scale = 1.0 / math.sqrt(mode_total)
    total_a = reduce_scatter(send_a, keep_a, size, block_rows)
    total_b = reduce_scatter(send_b, keep_b, size, block_rows)
    gathered = []
    for own, arrived in (total_a, total_b):
        here, there = mix(own, arrived, query_full, mix_full, out_full, scale, own_modes)
        block = jnp.concatenate([here, to_core(there)], axis=0)
        gathered.append(gather(block, size))
    output = inverse(place, table_back, gathered[0], None, series_count, half, 0, back_scale)
    return inverse(place, table_back, gathered[1], output, series_count, half, count, back_scale)


def solution(mesh):
    in_specs = (
        P(None, "tm", None),
        P(),
        P(None, "head"),
        P("tm", "head", None, None),
        P(None, "head"),
    )
    out_specs = P(None, "tm", "head")
    return jax.shard_map(body, mesh=mesh, in_specs=in_specs, out_specs=out_specs, check_vma=False)
```

```python
import functools
import math

import jax
import jax.numpy as jnp
from jax import lax
from jax.experimental import pallas as pl
from jax.experimental.pallas import tpu as pltpu
from jax.sharding import PartitionSpec as P

f32 = jnp.float32
bf16 = jnp.bfloat16
two_pi = 2.0 * math.pi


def in_vmem(shape, dtype):
    return pltpu.VMEM(shape, dtype)


def held(*arrays):
    return [pltpu.with_memory_space_constraint(array, pltpu.VMEM) for array in arrays]


def in_hbm(array):
    return pltpu.with_memory_space_constraint(array, pltpu.HBM)


def after(array, *others):
    return lax.optimization_barrier((array, *others))[0]


whole = pl.BlockSpec(memory_space=pltpu.VMEM)
small = pl.CostEstimate(flops=1000, bytes_accessed=1000, transcendentals=0)


def row_modes(place, core, modes_row, rows, own_modes, series_length):
    lanes = modes_row.shape[1]
    row = lax.broadcasted_iota(jnp.int32, (rows, lanes), 0)
    lane = lax.broadcasted_iota(jnp.int32, (rows, lanes), 1)
    block_rows = 2 * own_modes
    far = rows // block_rows // 4
    block = row // block_rows
    inside = row - block * block_rows
    quarter = block // far
    relative = (quarter // 2) * (1 + core) + (quarter % 2) * (2 - core) + 4 * (block % far)
    imaginary = inside // own_modes
    wanted = (place ^ relative) * own_modes + inside - imaginary * own_modes
    picked = jnp.where(lane == wanted, modes_row.astype(f32), 0.0)
    mode = jnp.sum(picked, axis=1, keepdims=True).astype(jnp.int32)
    return mode, imaginary[:, :1] * (series_length // 4)


def wave(phases, series_length):
    turns = phases.astype(f32) * (1.0 / series_length)
    quarters = jnp.floor(turns * 4.0 + 0.5)
    angle = (turns - quarters * 0.25) * two_pi
    square = angle * angle
    cosine = 1.0 + square * (-0.5 + square * (1 / 24 + square * (-1 / 720 + square * (1 / 40320))))
    sine = angle * (1.0 + square * (-1 / 6 + square * (1 / 120 + square * (-1 / 5040))))
    which = quarters.astype(jnp.int32)
    odd = which & 1 == 1
    cos_size = jnp.where(odd, sine, cosine)
    sin_size = jnp.where(odd, cosine, sine)
    cos_flip = (which == 1) | (which == 2)
    sin_flip = (which == 2) | (which == 3)
    return jnp.where(cos_flip, -cos_size, cos_size), jnp.where(sin_flip, -sin_size, sin_size)


def fill_table(modes_ref, table_ref, own_modes, series_length):
    rows, time_count = table_ref.shape
    place = lax.axis_index("tm")
    mode, shift = row_modes(place, lax.axis_index("head"), modes_ref[...], rows, own_modes, series_length)
    lane = lax.broadcasted_iota(jnp.int32, (rows, 128), 1)
    last = series_length - 1
    cos_a, sin_a = wave((mode * (place * time_count + lane * 128) + shift) & last, series_length)
    cos_b, sin_b = wave((mode * lane) & last, series_length)
    for piece in range(time_count // 128):
        value = cos_a[:, piece:piece + 1] * cos_b - sin_a[:, piece:piece + 1] * sin_b
        table_ref[:, piece * 128:piece * 128 + 128] = value.astype(bf16)


def forward_kernel(first, count, offset, half, own_modes, series_length, extra_ref, series_ref, *refs):
    if first:
        send_ref, keep_ref, table_ref, held, sems = refs
    else:
        send_ref, keep_ref, held, sems = refs
        table_ref = extra_ref
    base = lax.axis_index("head") * half + offset
    copies = [pltpu.make_async_copy(series_ref.at[base + b], held.at[b], sems.at[b]) for b in range(count)]
    for copy in copies:
        copy.start()
    if first:
        fill_table(extra_ref, table_ref, own_modes, series_length)
    middle = table_ref.shape[0] // 2
    for b in range(count):
        copies[b].wait()
        part = jnp.dot(table_ref[...], held[b], preferred_element_type=f32)
        send_ref[b] = part[middle:].astype(bf16)
        keep_ref[b] = part[:middle]


def forward(first, series, extra, count, offset, half, own_modes, series_length, rows):
    _, time_count, width = series.shape
    outs = [in_vmem((count, rows // 2, width), bf16), in_vmem((count, rows // 2, width), f32)]
    if first:
        outs.append(in_vmem((rows, time_count), bf16))
        extra = in_hbm(extra)
    else:
        extra, = held(extra)
    return pl.pallas_call(
        functools.partial(forward_kernel, first, count, offset, half, own_modes, series_length),
        out_shape=outs,
        in_specs=[whole, pl.BlockSpec(memory_space=pltpu.HBM)],
        out_specs=[whole] * len(outs),
        scratch_shapes=[pltpu.VMEM((count, time_count, width), bf16), pltpu.SemaphoreType.DMA((count,))],
        compiler_params=pltpu.CompilerParams(vmem_limit_bytes=16 * 2**20),
        cost_estimate=small,
        name="forward_first" if first else "forward_second",
    )(extra, in_hbm(series))


def onward_kernel(keep_ref, arrived_ref, out_ref):
    middle = keep_ref.shape[1] // 2
    out_ref[...] = (keep_ref[:, middle:] + arrived_ref[:, middle:].astype(f32)).astype(bf16)


def onward(keep, arrived):
    count, rows, width = keep.shape
    return pl.pallas_call(
        onward_kernel,
        out_shape=in_vmem((count, rows // 2, width), bf16),
        in_specs=[whole] * 2,
        out_specs=whole,
        compiler_params=pltpu.CompilerParams(vmem_limit_bytes=16 * 2**20),
        cost_estimate=small,
        name="sum_onward",
    )(*held(keep, arrived))


def total_kernel(block_rows, keep_ref, arrived_ref, second_ref, own_ref, *far_refs):
    middle = second_ref.shape[1]
    total = keep_ref[:, :middle] + arrived_ref[:, :middle].astype(f32) + second_ref[...].astype(f32)
    own_ref[...] = total[:, :block_rows]
    for index, ref in enumerate(far_refs):
        ref[...] = total[:, (index + 1) * block_rows:(index + 2) * block_rows].astype(bf16)


def total_rows(keep, arrived, second, block_rows):
    count, rows, width = second.shape
    if block_rows % 16:
        total = keep[:, :rows] + arrived[:, :rows].astype(f32) + second.astype(f32)
        parts = [total[:, start:start + block_rows] for start in range(0, rows, block_rows)]
        return parts[0], [part.astype(bf16) for part in parts[1:]]
    share = (count, block_rows, width)
    parts = pl.pallas_call(
        functools.partial(total_kernel, block_rows),
        out_shape=[in_vmem(share, f32)] + [in_vmem(share, bf16)] * (rows // block_rows - 1),
        in_specs=[whole] * 3,
        out_specs=[whole] * (rows // block_rows),
        compiler_params=pltpu.CompilerParams(vmem_limit_bytes=16 * 2**20),
        cost_estimate=small,
        name="sum_total",
    )(*held(keep, arrived, second))
    return parts[0], parts[1:]


def prepare_kernel(weight_ref, table_ref, *out_refs):
    modes, heads, size, width = weight_ref.shape
    negative = lax.broadcasted_iota(jnp.int32, (size, width), 1) < size
    for m in range(modes):
        for h in range(heads):
            weight = weight_ref[m, h]
            turned = pltpu.roll(weight, size, 1)
            start = 2 * size * m
            out_refs[h][start:start + size] = weight.astype(bf16)
            out_refs[h][start + size:start + 2 * size] = jnp.where(negative, -turned, turned).astype(bf16)
    out_refs[heads][...] = table_ref[...].T


def prepare(weight, table):
    modes, heads, size, width = weight.shape
    outs = pl.pallas_call(
        prepare_kernel,
        out_shape=[in_vmem((modes * 2 * size, width), bf16)] * heads + [in_vmem(table.shape[::-1], bf16)],
        in_specs=[whole] * 2,
        out_specs=[whole] * (heads + 1),
        compiler_params=pltpu.CompilerParams(vmem_limit_bytes=16 * 2**20),
        cost_estimate=small,
        name="prepare_mix",
    )(in_hbm(weight), *held(table))
    return outs[:heads], outs[heads]


def split_rows(value):
    high = value.astype(bf16)
    low = (value - high.astype(f32)).astype(bf16)
    return jnp.concatenate([high, low], axis=0)


def fold_rows(value):
    half = value.shape[0] // 2
    return value[:half] + value[half:]


def mix_kernel(scale, own_modes, arrivals, own_ref, *refs):
    arrived = refs[:arrivals]
    query_refs, out_weight_refs, mix_refs = refs[arrivals:arrivals + 2], refs[arrivals + 2:arrivals + 4], refs[arrivals + 4:-2]
    here_ref, there_ref = refs[-2:]
    total = own_ref[...]
    for ref in arrived:
        total = total + ref[...].astype(f32)
    total = total * scale
    count, _, width = total.shape
    rows = count * own_modes
    half = width // 2
    core = lax.axis_index("head")
    pieces = split_rows(jnp.concatenate(
        [total[:, :own_modes].reshape(rows, width), total[:, own_modes:].reshape(rows, width)], axis=0
    ))
    lower = lax.broadcasted_iota(jnp.int32, (rows, 128), 1) < 64
    row_mode = lax.broadcasted_iota(jnp.int32, (2 * rows, 128), 0) % own_modes
    mixed = []
    for group, query_ref in enumerate(query_refs):
        queries = fold_rows(jnp.dot(pieces, query_ref[...], preferred_element_type=f32))
        mixed_real, mixed_imag = [], []
        for pair in range(half // 128):
            columns = slice(pair * 128, pair * 128 + 128)
            real, imag = queries[:rows, columns], queries[rows:, columns]
            both = [
                jnp.where(lower, real, pltpu.roll(imag, 64, 1)),
                jnp.where(lower, pltpu.roll(real, 64, 1), imag),
            ]
            heads = []
            for which in range(2):
                spread = split_rows(both[which])
                zero = jnp.zeros_like(spread)
                spread = jnp.concatenate([jnp.where(row_mode == k, spread, zero) for k in range(own_modes)], axis=1)
                mix_ref = mix_refs[group * (half // 64) + 2 * pair + which]
                heads.append(fold_rows(jnp.dot(spread, mix_ref[...], preferred_element_type=f32)))
            mixed_real.append(jnp.where(lower, heads[0], pltpu.roll(heads[1], 64, 1)))
            mixed_imag.append(jnp.where(lower, pltpu.roll(heads[0], 64, 1), heads[1]))
        both = jnp.concatenate([jnp.concatenate(mixed_real, axis=1), jnp.concatenate(mixed_imag, axis=1)], axis=0)
        mixed.append(split_rows(both))
    first = jnp.where(core == 0, mixed[0], mixed[1])
    second = jnp.where(core == 0, mixed[1], mixed[0])
    both = jnp.concatenate([first, second], axis=1)
    for weight_ref, out_ref in zip(out_weight_refs, (here_ref, there_ref)):
        result = fold_rows(jnp.dot(both, weight_ref[...], preferred_element_type=f32)).astype(bf16)
        out_ref[...] = jnp.concatenate(
            [result[:rows].reshape(count, own_modes, half), result[rows:].reshape(count, own_modes, half)], axis=1
        )


def mix(own, arrived, queries, outs, mixes, scale, own_modes):
    count, block_rows, width = own.shape
    here = width // 2
    if own_modes % 8 == 0:
        shape = in_vmem((count, block_rows, here), bf16)
        return pl.pallas_call(
            functools.partial(mix_kernel, scale, own_modes, len(arrived)),
            out_shape=[shape, shape],
            in_specs=[whole] * (5 + len(arrived) + len(mixes)),
            out_specs=[whole, whole],
            compiler_params=pltpu.CompilerParams(vmem_limit_bytes=16 * 2**20),
            cost_estimate=small,
            name="mix_modes",
        )(*held(own, *arrived, *queries, *outs, *mixes))
    core = lax.axis_index("head")
    highest = lax.Precision.HIGHEST
    total = (own + sum(piece.astype(f32) for piece in arrived)) * scale
    mixed = []
    heads = len(mixes) // 2
    for group, query in enumerate(queries):
        weights = jnp.stack(mixes[group * heads:(group + 1) * heads])
        projected = jnp.einsum("brf,fg->brg", total, query.astype(f32), precision=highest)
        projected = projected.reshape(count, 2, own_modes, heads, 64)
        weights = weights.reshape(heads, own_modes, 2, 64, 2, 64).astype(f32)
        part = jnp.einsum("brmhi,hmriso->bsmho", projected, weights, precision=highest)
        mixed.append(part.reshape(count, block_rows, here))
    mixed = jnp.concatenate(mixed, axis=2)
    results = []
    for out_weight in outs:
        rolled = jnp.where(core == 0, out_weight, jnp.roll(out_weight, here, axis=0)).astype(f32)
        results.append(jnp.einsum("brf,fg->brg", mixed, rolled, precision=highest).astype(bf16))
    return results


def inverse_kernel(half, offset, table_ref, *refs):
    pieces, (out_ref, held, sems) = refs[:4], refs[-3:]
    count = held.shape[0]
    own = count // 2
    core = lax.axis_index("head")
    copies = []
    for b in range(count):
        spectra = jnp.concatenate([piece[b] for piece in pieces], axis=0)
        held[b] = jnp.dot(table_ref[...], spectra, preferred_element_type=f32).astype(bf16)
        index = (core ^ (b // own)) * half + offset + b % own
        copies.append(pltpu.make_async_copy(held.at[b], out_ref.at[index], sems.at[b]))
        copies[-1].start()
    for copy in copies:
        copy.wait()


def inverse(table, pieces, previous, series_count, half, offset):
    time_count, rows = table.shape
    count, _, width = pieces[0].shape
    in_specs = [whole] * 5
    args = held(table, *pieces)
    aliases = {}
    if previous is not None:
        in_specs.append(pl.BlockSpec(memory_space=pltpu.HBM))
        aliases = {len(args): 0}
        args.append(in_hbm(previous))
    return pl.pallas_call(
        functools.partial(inverse_kernel, half, offset),
        out_shape=pltpu.HBM((series_count, time_count, width), bf16),
        in_specs=in_specs,
        out_specs=pl.BlockSpec(memory_space=pltpu.HBM),
        scratch_shapes=[pltpu.VMEM((count, time_count, width), bf16), pltpu.SemaphoreType.DMA((count,))],
        input_output_aliases=aliases,
        compiler_params=pltpu.CompilerParams(vmem_limit_bytes=16 * 2**20),
        cost_estimate=small,
        name="inverse_first" if previous is None else "inverse_second",
    )(*args)


def to_devices(value, masks, size):
    pairs = [(2 * i + c, 2 * (i ^ masks[c]) + c) for i in range(size) for c in range(2)]
    return lax.ppermute(value, ("tm", "head"), pairs)


going_first, going_second = (1, 2), (2, 1)


def to_core(value):
    return lax.ppermute(value, "head", [(0, 1), (1, 0)])


def send_far(parts, size):
    return [to_devices(parts[z - 1], (4 * z, 4 * z), size) for z in range(len(parts), 0, -1)]


def join_kernel(*refs):
    out_ref = refs[-1]
    rows = refs[0].shape[1]
    for index, ref in enumerate(refs[:-1]):
        out_ref[:, index * rows:(index + 1) * rows] = ref[...]


def gather_far(block, size):
    far = [to_devices(block, (4 * z, 4 * z), size) for z in range(size // 4 - 1, 0, -1)]
    pieces = [block] + far[::-1]
    count, rows, width = block.shape
    if rows % 16:
        return jnp.concatenate(pieces, axis=1)
    return pl.pallas_call(
        join_kernel,
        out_shape=in_vmem((count, rows * len(pieces), width), bf16),
        in_specs=[whole] * len(pieces),
        out_specs=whole,
        compiler_params=pltpu.CompilerParams(vmem_limit_bytes=16 * 2**20),
        cost_estimate=small,
        name="join_rows",
    )(*held(*pieces))


def body(series, modes, query_weight, mix_weight, out_weight):
    series_count, shard_rows, width = series.shape
    own_modes, heads_here, head_size, _ = mix_weight.shape
    mode_total = modes.shape[0]
    size = lax.axis_size("tm")
    series_length = size * shard_rows
    rows = 2 * mode_total
    half = series_count // 2
    count_a = half // 2
    count_b = half - count_a

    send_a, keep_a, table = forward(
        True, series, modes[None, :], count_a, 0, half, own_modes, series_length, rows
    )
    send_b, keep_b = forward(False, series, table, count_b, count_a, half, own_modes, series_length, rows)
    block_rows = 2 * own_modes
    scale = 1.0 / math.sqrt(series_length * mode_total)
    arrived_a = to_devices(send_a, going_first, size)
    arrived_b = to_devices(send_b, going_first, size)

    mix_here, table_back = prepare(mix_weight, table)
    query_weight, out_weight = after(query_weight, table), after(out_weight, table)
    weights = [[query_weight, to_core(query_weight)], [out_weight, to_core(out_weight)]]
    weights.append([*mix_here, *(to_core(w) for w in mix_here)])

    onward_a = onward(after(keep_a, keep_b, mix_here[0]), arrived_a)
    second_a = to_devices(onward_a, going_second, size)
    onward_b = onward(after(keep_b, onward_a), arrived_b)
    second_b = to_devices(onward_b, going_second, size)
    own_a, far_a = total_rows(after(keep_a, onward_b), arrived_a, second_a, block_rows)
    far_a = send_far(far_a, size)
    own_b, far_b = total_rows(after(keep_b, own_a), arrived_b, second_b, block_rows)
    far_b = send_far(far_b, size)

    here_a, there_a = mix(after(own_a, own_b), far_a, *weights, scale, own_modes)
    block_a = jnp.concatenate([here_a, to_core(there_a)], axis=0)
    here_b, there_b = mix(after(own_b, block_a), far_b, *weights, scale, own_modes)
    block_b = jnp.concatenate([here_b, to_core(there_b)], axis=0)
    rows_a = after(gather_far(block_a, size), block_b)
    second_a = to_devices(rows_a, going_second, size)
    first_a = to_devices(rows_a, going_first, size)
    both_a = to_devices(second_a, going_first, size)
    rows_b = gather_far(block_b, size)
    second_b = to_devices(rows_b, going_second, size)
    first_b = to_devices(rows_b, going_first, size)
    pieces_a = [after(rows_a, second_b), second_a, first_a, both_a]
    output = inverse(table_back, pieces_a, None, series_count, half, 0)
    both_b = to_devices(after(second_b, first_a), going_first, size)
    return inverse(table_back, [rows_b, second_b, first_b, both_b], output, series_count, half, count_a)


def solution(mesh):
    in_specs = (
        P(None, "tm", None),
        P(),
        P(None, "head"),
        P("tm", "head", None, None),
        P(None, "head"),
    )
    out_specs = P(None, "tm", "head")
    return jax.shard_map(body, mesh=mesh, in_specs=in_specs, out_specs=out_specs, check_vma=False)
```

```python
import functools
import math

import jax
import jax.numpy as jnp
from jax import lax
from jax.experimental import pallas as pl
from jax.experimental.pallas import tpu as pltpu
from jax.sharding import PartitionSpec as P

f32 = jnp.float32
bf16 = jnp.bfloat16
two_pi = 2.0 * math.pi


ahead = pl.CostEstimate(flops=3 * 10**9, bytes_accessed=1000, transcendentals=0)


def in_vmem(shape, dtype):
    return pltpu.VMEM(shape, dtype)


def held(*arrays):
    return [pltpu.with_memory_space_constraint(array, pltpu.VMEM) for array in arrays]


def in_hbm(array):
    return pltpu.with_memory_space_constraint(array, pltpu.HBM)


def after(array, *others):
    return lax.optimization_barrier((array, *others))[0]


whole = pl.BlockSpec(memory_space=pltpu.VMEM)
small = pl.CostEstimate(flops=1000, bytes_accessed=1000, transcendentals=0)


def row_modes(place, core, modes_row, rows, own_modes, series_length):
    lanes = modes_row.shape[1]
    row = lax.broadcasted_iota(jnp.int32, (rows, lanes), 0)
    lane = lax.broadcasted_iota(jnp.int32, (rows, lanes), 1)
    block_rows = 2 * own_modes
    far = rows // block_rows // 4
    block = row // block_rows
    inside = row - block * block_rows
    quarter = block // far
    relative = (quarter // 2) * (1 + core) + (quarter % 2) * (2 - core) + 4 * (block % far)
    imaginary = inside // own_modes
    wanted = (place ^ relative) * own_modes + inside - imaginary * own_modes
    picked = jnp.where(lane == wanted, modes_row.astype(f32), 0.0)
    mode = jnp.sum(picked, axis=1, keepdims=True).astype(jnp.int32)
    return mode, imaginary[:, :1] * (series_length // 4)


def wave(phases, series_length):
    turns = phases.astype(f32) * (1.0 / series_length)
    quarters = jnp.floor(turns * 4.0 + 0.5)
    angle = (turns - quarters * 0.25) * two_pi
    square = angle * angle
    cosine = 1.0 + square * (-0.5 + square * (1 / 24 + square * (-1 / 720 + square * (1 / 40320))))
    sine = angle * (1.0 + square * (-1 / 6 + square * (1 / 120 + square * (-1 / 5040))))
    which = quarters.astype(jnp.int32)
    odd = which & 1 == 1
    cos_size = jnp.where(odd, sine, cosine)
    sin_size = jnp.where(odd, cosine, sine)
    cos_flip = (which == 1) | (which == 2)
    sin_flip = (which == 2) | (which == 3)
    return jnp.where(cos_flip, -cos_size, cos_size), jnp.where(sin_flip, -sin_size, sin_size)


def fill_table(modes_ref, table_ref, own_modes, series_length):
    rows, time_count = table_ref.shape
    place = lax.axis_index("tm")
    mode, shift = row_modes(place, lax.axis_index("head"), modes_ref[...], rows, own_modes, series_length)
    lane = lax.broadcasted_iota(jnp.int32, (rows, 128), 1)
    last = series_length - 1
    cos_a, sin_a = wave((mode * (place * time_count + lane * 128) + shift) & last, series_length)
    cos_b, sin_b = wave((mode * lane) & last, series_length)
    for piece in range(time_count // 128):
        value = cos_a[:, piece:piece + 1] * cos_b - sin_a[:, piece:piece + 1] * sin_b
        table_ref[:, piece * 128:piece * 128 + 128] = value.astype(bf16)


def forward_kernel(first, count, offset, half, own_modes, series_length, extra_ref, series_ref, *refs):
    if first:
        send_ref, keep_ref, table_ref, held, sems = refs
    else:
        corner_ref, side_ref, keep_ref, held, sems = refs
        table_ref = extra_ref
    base = lax.axis_index("head") * half + offset
    copies = [pltpu.make_async_copy(series_ref.at[base + b], held.at[b], sems.at[b]) for b in range(count)]
    for copy in copies:
        copy.start()
    if first:
        fill_table(extra_ref, table_ref, own_modes, series_length)
    middle = table_ref.shape[0] // 2
    for b in range(count):
        copies[b].wait()
        part = jnp.dot(table_ref[...], held[b], preferred_element_type=f32)
        if first:
            send_ref[b] = part[middle:].astype(bf16)
        else:
            side_ref[b] = part[middle:middle + middle // 2].astype(bf16)
            corner_ref[b] = part[middle + middle // 2:].astype(bf16)
        keep_ref[b] = part[:middle]


def forward(first, series, extra, count, offset, half, own_modes, series_length, rows):
    _, time_count, width = series.shape
    sends = [in_vmem((count, rows // 2, width), bf16)] if first else [in_vmem((count, rows // 4, width), bf16)] * 2
    outs = sends + [in_vmem((count, rows // 2, width), f32)]
    if first:
        outs.append(in_vmem((rows, time_count), bf16))
        extra = in_hbm(extra)
    else:
        extra, = held(extra)
    return pl.pallas_call(
        functools.partial(forward_kernel, first, count, offset, half, own_modes, series_length),
        out_shape=outs,
        in_specs=[whole, pl.BlockSpec(memory_space=pltpu.HBM)],
        out_specs=[whole] * len(outs),
        scratch_shapes=[pltpu.VMEM((count, time_count, width), bf16), pltpu.SemaphoreType.DMA((count,))],
        compiler_params=pltpu.CompilerParams(vmem_limit_bytes=16 * 2**20),
        cost_estimate=small,
        name="forward_first" if first else "forward_second",
    )(extra, in_hbm(series))


def onward_kernel(keep_ref, arrived_ref, out_ref):
    middle = keep_ref.shape[1] // 2
    out_ref[...] = (keep_ref[:, middle:] + arrived_ref[:, -middle:].astype(f32)).astype(bf16)


def onward(keep, arrived, cost=small):
    count, rows, width = keep.shape
    return pl.pallas_call(
        onward_kernel,
        out_shape=in_vmem((count, rows // 2, width), bf16),
        in_specs=[whole] * 2,
        out_specs=whole,
        compiler_params=pltpu.CompilerParams(vmem_limit_bytes=16 * 2**20),
        cost_estimate=cost,
        name="sum_onward",
    )(*held(keep, arrived))


def total_kernel(block_rows, keep_ref, arrived_ref, second_ref, own_ref, *far_refs):
    middle = second_ref.shape[1]
    total = keep_ref[:, :middle] + arrived_ref[:, :middle].astype(f32) + second_ref[...].astype(f32)
    own_ref[...] = total[:, :block_rows]
    for index, ref in enumerate(far_refs):
        ref[...] = total[:, (index + 1) * block_rows:(index + 2) * block_rows].astype(bf16)


def total_rows(keep, arrived, second, block_rows):
    count, rows, width = second.shape
    if block_rows % 16:
        total = keep[:, :rows] + arrived[:, :rows].astype(f32) + second.astype(f32)
        parts = [total[:, start:start + block_rows] for start in range(0, rows, block_rows)]
        return parts[0], [part.astype(bf16) for part in parts[1:]]
    share = (count, block_rows, width)
    parts = pl.pallas_call(
        functools.partial(total_kernel, block_rows),
        out_shape=[in_vmem(share, f32)] + [in_vmem(share, bf16)] * (rows // block_rows - 1),
        in_specs=[whole] * 3,
        out_specs=[whole] * (rows // block_rows),
        compiler_params=pltpu.CompilerParams(vmem_limit_bytes=16 * 2**20),
        cost_estimate=small,
        name="sum_total",
    )(*held(keep, arrived, second))
    return parts[0], parts[1:]


mix_arrays = 2


def prepare_kernel(weight_ref, query_ref, out_weight_ref, table_ref, *refs):
    modes, heads, size, width = weight_ref.shape
    negative = lax.broadcasted_iota(jnp.int32, (size, width), 1) < size
    for h in range(heads):
        out_ref = refs[h * mix_arrays // heads]
        start = h % (heads // mix_arrays) * modes * 2 * size
        for m in range(modes):
            weight = weight_ref[m, h]
            turned = pltpu.roll(weight, size, 1)
            out_ref[start:start + size] = weight.astype(bf16)
            out_ref[start + size:start + 2 * size] = jnp.where(negative, -turned, turned).astype(bf16)
            start += 2 * size
    out_ref, back_ref = refs[mix_arrays:]
    start = 0
    for ref in (query_ref, out_weight_ref):
        depth, columns = ref.shape
        for first in range(0, columns, width):
            out_ref[start:start + depth] = ref[:, first:first + width]
            start += depth
    back_ref[...] = table_ref[...].T


def prepare(weight, query, out_weight, table):
    modes, heads, size, width = weight.shape
    mixes = in_vmem((modes * heads // mix_arrays * 2 * size, width), bf16)
    outs = pl.pallas_call(
        prepare_kernel,
        out_shape=[mixes] * mix_arrays + [in_vmem((2 * query.size // width, width), bf16), in_vmem(table.shape[::-1], bf16)],
        in_specs=[whole] * 4,
        out_specs=[whole] * (mix_arrays + 2),
        compiler_params=pltpu.CompilerParams(vmem_limit_bytes=16 * 2**20),
        cost_estimate=small,
        name="prepare_weights",
    )(in_hbm(weight), in_hbm(query), in_hbm(out_weight), *held(table))
    return outs[:-1], outs[-1]


def packed_parts(packed, heads, depth):
    weights = packed[-1][...]
    mixes = []
    for array in packed[:-1]:
        step = array.shape[0] * mix_arrays // heads
        mixes += [array[start:start + step] for start in range(0, array.shape[0], step)]
    columns = [weights[start:start + depth] for start in range(0, weights.shape[0], depth)]
    middle = len(columns) // 2
    return mixes, jnp.concatenate(columns[:middle], axis=1), jnp.concatenate(columns[middle:], axis=1)


def split_rows(value):
    high = value.astype(bf16)
    low = (value - high.astype(f32)).astype(bf16)
    return jnp.concatenate([high, low], axis=0)


def fold_rows(value):
    half = value.shape[0] // 2
    return value[:half] + value[half:]


def mix_kernel(scale, own_modes, arrivals, own_ref, *refs):
    arrived = refs[:arrivals]
    packed_refs, (here_ref, there_ref) = refs[arrivals:-2], refs[-2:]
    each = len(packed_refs) // 2
    total = own_ref[...]
    for ref in arrived:
        total = total + ref[...].astype(f32)
    total = total * scale
    count, _, width = total.shape
    rows = count * own_modes
    half = width // 2
    core = lax.axis_index("head")
    pieces = split_rows(jnp.concatenate(
        [total[:, :own_modes].reshape(rows, width), total[:, own_modes:].reshape(rows, width)], axis=0
    ))
    lower = lax.broadcasted_iota(jnp.int32, (rows, 128), 1) < 64
    row_mode = lax.broadcasted_iota(jnp.int32, (2 * rows, 128), 0) % own_modes
    mixed, out_weights = [], []
    for packed in (packed_refs[:each], packed_refs[each:]):
        mixes, query, out_weight = packed_parts(packed, half // 64, width)
        out_weights.append(out_weight)
        queries = fold_rows(jnp.dot(pieces, query, preferred_element_type=f32))
        mixed_real, mixed_imag = [], []
        for pair in range(half // 128):
            columns = slice(pair * 128, pair * 128 + 128)
            real, imag = queries[:rows, columns], queries[rows:, columns]
            both = [
                jnp.where(lower, real, pltpu.roll(imag, 64, 1)),
                jnp.where(lower, pltpu.roll(real, 64, 1), imag),
            ]
            heads = []
            for which in range(2):
                spread = split_rows(both[which])
                zero = jnp.zeros_like(spread)
                spread = jnp.concatenate([jnp.where(row_mode == k, spread, zero) for k in range(own_modes)], axis=1)
                heads.append(fold_rows(jnp.dot(spread, mixes[2 * pair + which], preferred_element_type=f32)))
            mixed_real.append(jnp.where(lower, heads[0], pltpu.roll(heads[1], 64, 1)))
            mixed_imag.append(jnp.where(lower, pltpu.roll(heads[0], 64, 1), heads[1]))
        both = jnp.concatenate([jnp.concatenate(mixed_real, axis=1), jnp.concatenate(mixed_imag, axis=1)], axis=0)
        mixed.append(split_rows(both))
    first = jnp.where(core == 0, mixed[0], mixed[1])
    second = jnp.where(core == 0, mixed[1], mixed[0])
    both = jnp.concatenate([first, second], axis=1)
    for out_weight, out_ref in zip(out_weights, (here_ref, there_ref)):
        result = fold_rows(jnp.dot(both, out_weight, preferred_element_type=f32)).astype(bf16)
        out_ref[...] = jnp.concatenate(
            [result[:rows].reshape(count, own_modes, half), result[rows:].reshape(count, own_modes, half)], axis=1
        )


def mix(own, arrived, packed, scale, own_modes):
    count, block_rows, width = own.shape
    here = width // 2
    if own_modes % 8 == 0:
        shape = in_vmem((count, block_rows, here), bf16)
        return pl.pallas_call(
            functools.partial(mix_kernel, scale, own_modes, len(arrived)),
            out_shape=[shape, shape],
            in_specs=[whole] * (1 + len(arrived) + 2 * len(packed[0])),
            out_specs=[whole, whole],
            compiler_params=pltpu.CompilerParams(vmem_limit_bytes=16 * 2**20),
            cost_estimate=small,
            name="mix_modes",
        )(*held(own, *arrived, *packed[0], *packed[1]))
    core = lax.axis_index("head")
    highest = lax.Precision.HIGHEST
    total = (own + sum(piece.astype(f32) for piece in arrived)) * scale
    heads = here // 64
    mixed, results = [], []
    for side in packed:
        mixes, query, _ = packed_parts(side, heads, width)
        projected = jnp.einsum("brf,fg->brg", total, query.astype(f32), precision=highest)
        projected = projected.reshape(count, 2, own_modes, heads, 64)
        weights = jnp.stack(mixes).reshape(heads, own_modes, 2, 64, 2, 64).astype(f32)
        part = jnp.einsum("brmhi,hmriso->bsmho", projected, weights, precision=highest)
        mixed.append(part.reshape(count, block_rows, here))
    mixed = jnp.concatenate(mixed, axis=2)
    mixed = jnp.where(core == 0, mixed, jnp.roll(mixed, here, axis=2))
    for side in packed:
        out_weight = packed_parts(side, heads, width)[2].astype(f32)
        results.append(jnp.einsum("brf,fg->brg", mixed, out_weight, precision=highest).astype(bf16))
    return results


def inverse_kernel(half, offset, table_ref, *refs):
    pieces, (out_ref, held, sems) = refs[:4], refs[-3:]
    count = held.shape[0]
    own = count // 2
    core = lax.axis_index("head")
    copies = []
    for b in range(count):
        spectra = jnp.concatenate([piece[b] for piece in pieces], axis=0)
        held[b] = jnp.dot(table_ref[...], spectra, preferred_element_type=f32).astype(bf16)
        index = (core ^ (b // own)) * half + offset + b % own
        copies.append(pltpu.make_async_copy(held.at[b], out_ref.at[index], sems.at[b]))
        copies[-1].start()
    for copy in copies:
        copy.wait()


def inverse(table, pieces, previous, series_count, half, offset):
    time_count, rows = table.shape
    count, _, width = pieces[0].shape
    in_specs = [whole] * 5
    args = held(table, *pieces)
    aliases = {}
    if previous is not None:
        in_specs.append(pl.BlockSpec(memory_space=pltpu.HBM))
        aliases = {len(args): 0}
        args.append(in_hbm(previous))
    return pl.pallas_call(
        functools.partial(inverse_kernel, half, offset),
        out_shape=pltpu.HBM((series_count, time_count, width), bf16),
        in_specs=in_specs,
        out_specs=pl.BlockSpec(memory_space=pltpu.HBM),
        scratch_shapes=[pltpu.VMEM((count, time_count, width), bf16), pltpu.SemaphoreType.DMA((count,))],
        input_output_aliases=aliases,
        compiler_params=pltpu.CompilerParams(vmem_limit_bytes=16 * 2**20),
        cost_estimate=small,
        name="inverse_first" if previous is None else "inverse_second",
    )(*args)


def to_devices(value, masks, size):
    pairs = [(2 * i + c, 2 * (i ^ masks[c]) + c) for i in range(size) for c in range(2)]
    return lax.ppermute(value, ("tm", "head"), pairs)


going_first, going_second = (1, 2), (2, 1)


def to_core(value):
    return lax.ppermute(value, "head", [(0, 1), (1, 0)])


def send_far(parts, size):
    return [to_devices(parts[z - 1], (4 * z, 4 * z), size) for z in range(len(parts), 0, -1)]


def join_kernel(*refs):
    out_ref = refs[-1]
    rows = refs[0].shape[1]
    for index, ref in enumerate(refs[:-1]):
        out_ref[:, index * rows:(index + 1) * rows] = ref[...]


def gather_far(block, size):
    far = [to_devices(block, (4 * z, 4 * z), size) for z in range(size // 4 - 1, 0, -1)]
    pieces = [block] + far[::-1]
    count, rows, width = block.shape
    if rows % 16:
        return jnp.concatenate(pieces, axis=1)
    return pl.pallas_call(
        join_kernel,
        out_shape=in_vmem((count, rows * len(pieces), width), bf16),
        in_specs=[whole] * len(pieces),
        out_specs=whole,
        compiler_params=pltpu.CompilerParams(vmem_limit_bytes=16 * 2**20),
        cost_estimate=small,
        name="join_rows",
    )(*held(*pieces))


def body(series, modes, query_weight, mix_weight, out_weight):
    series_count, shard_rows, width = series.shape
    own_modes, heads_here, head_size, _ = mix_weight.shape
    mode_total = modes.shape[0]
    size = lax.axis_size("tm")
    series_length = size * shard_rows
    rows = 2 * mode_total
    half = series_count // 2
    count_a = half // 2
    count_b = half - count_a

    send_a, keep_a, table = forward(
        True, series, modes[None, :], count_a, 0, half, own_modes, series_length, rows
    )
    corner_b, side_b, keep_b = forward(False, series, table, count_b, count_a, half, own_modes, series_length, rows)
    block_rows = 2 * own_modes
    scale = 1.0 / math.sqrt(series_length * mode_total)
    arrived_a = to_devices(send_a, going_first, size)
    corner_b = to_devices(corner_b, going_first, size)

    packed, table_back = prepare(after(mix_weight, keep_b), query_weight, out_weight, table)
    packed = [packed, [to_core(array) for array in packed]]

    onward_a = onward(after(keep_a, keep_b, *packed[0]), arrived_a)
    second_a = to_devices(onward_a, going_second, size)
    onward_b = onward(after(keep_b, onward_a), corner_b, ahead)
    second_b = to_devices(onward_b, going_second, size)
    side_b = to_devices(after(side_b, onward_b), going_first, size)
    own_a, far_a = total_rows(after(keep_a, onward_b, *packed[1]), arrived_a, second_a, block_rows)
    far_a = send_far(far_a, size)
    own_b, far_b = total_rows(after(keep_b, own_a), side_b, second_b, block_rows)
    far_b = send_far(far_b, size)

    here_a, there_a = mix(after(own_a, own_b), far_a, packed, scale, own_modes)
    block_a = jnp.concatenate([here_a, to_core(there_a)], axis=0)
    here_b, there_b = mix(after(own_b, block_a), far_b, packed, scale, own_modes)
    block_b = jnp.concatenate([here_b, to_core(there_b)], axis=0)
    rows_a = after(gather_far(block_a, size), block_b)
    second_a = to_devices(rows_a, going_second, size)
    first_a = to_devices(rows_a, going_first, size)
    both_a = to_devices(second_a, going_first, size)
    rows_b = gather_far(block_b, size)
    second_b = to_devices(rows_b, going_second, size)
    first_b = to_devices(rows_b, going_first, size)
    pieces_a = [after(rows_a, second_b), second_a, first_a, both_a]
    output = inverse(table_back, pieces_a, None, series_count, half, 0)
    both_b = to_devices(after(second_b, first_a), going_first, size)
    return inverse(table_back, [rows_b, second_b, first_b, both_b], output, series_count, half, count_a)


def solution(mesh):
    in_specs = (
        P(None, "tm", None),
        P(),
        P(None, "head"),
        P("tm", "head", None, None),
        P(None, "head"),
    )
    out_specs = P(None, "tm", "head")
    return jax.shard_map(body, mesh=mesh, in_specs=in_specs, out_specs=out_specs, check_vma=False)
```

```python
import functools
import math

import jax
import jax.numpy as jnp
from jax import lax
from jax.experimental import pallas as pl
from jax.experimental.pallas import tpu as pltpu
from jax.sharding import PartitionSpec as P

f32 = jnp.float32
bf16 = jnp.bfloat16
two_pi = 2.0 * math.pi


ahead = pl.CostEstimate(flops=3 * 10**9, bytes_accessed=1000, transcendentals=0)


def in_vmem(shape, dtype):
    return pltpu.VMEM(shape, dtype)


def held(*arrays):
    return [pltpu.with_memory_space_constraint(array, pltpu.VMEM) for array in arrays]


def in_hbm(array):
    return pltpu.with_memory_space_constraint(array, pltpu.HBM)


def after(array, *others):
    return lax.optimization_barrier((array, *others))[0]


whole = pl.BlockSpec(memory_space=pltpu.VMEM)
small = pl.CostEstimate(flops=1000, bytes_accessed=1000, transcendentals=0)


def row_modes(place, core, modes_row, rows, own_modes, series_length):
    lanes = modes_row.shape[1]
    row = lax.broadcasted_iota(jnp.int32, (rows, lanes), 0)
    lane = lax.broadcasted_iota(jnp.int32, (rows, lanes), 1)
    far = rows // own_modes // 8
    mode_bits, far_bits = own_modes.bit_length() - 1, far.bit_length() - 1
    block = row >> (mode_bits + 1)
    quarter = block >> far_bits
    relative = ((quarter >> 1) << core) + ((quarter & 1) << (1 - core)) + 4 * (block & (far - 1))
    imaginary = (row >> mode_bits) & 1
    wanted = ((place ^ relative) << mode_bits) + (row & (own_modes - 1))
    picked = jnp.where(lane == wanted, modes_row.astype(f32), 0.0)
    mode = jnp.sum(picked, axis=1, keepdims=True).astype(jnp.int32)
    return mode, imaginary[:, :1] * (series_length // 4)


def wave(phases, series_length):
    turns = phases.astype(f32) * (1.0 / series_length)
    quarters = jnp.floor(turns * 4.0 + 0.5)
    angle = (turns - quarters * 0.25) * two_pi
    square = angle * angle
    cosine = 1.0 + square * (-0.5 + square * (1 / 24 + square * (-1 / 720 + square * (1 / 40320))))
    sine = angle * (1.0 + square * (-1 / 6 + square * (1 / 120 + square * (-1 / 5040))))
    which = quarters.astype(jnp.int32)
    odd = which & 1 == 1
    cos_size = jnp.where(odd, sine, cosine)
    sin_size = jnp.where(odd, cosine, sine)
    cos_flip = (which == 1) | (which == 2)
    sin_flip = (which == 2) | (which == 3)
    return jnp.where(cos_flip, -cos_size, cos_size), jnp.where(sin_flip, -sin_size, sin_size)


def fill_table(modes_ref, table_ref, own_modes, series_length):
    rows, time_count = table_ref.shape
    place = lax.axis_index("tm")
    mode, shift = row_modes(place, lax.axis_index("head"), modes_ref[...], rows, own_modes, series_length)
    lane = lax.broadcasted_iota(jnp.int32, (rows, 128), 1)
    last = series_length - 1
    cos_a, sin_a = wave((mode * (place * time_count + lane * 128) + shift) & last, series_length)
    cos_b, sin_b = wave((mode * lane) & last, series_length)
    for piece in range(time_count // 128):
        value = cos_a[:, piece:piece + 1] * cos_b - sin_a[:, piece:piece + 1] * sin_b
        table_ref[:, piece * 128:piece * 128 + 128] = value.astype(bf16)


def forward_kernel(first, count, offset, half, own_modes, series_length, extra_ref, series_ref, *refs):
    if first:
        corner_ref, side_ref, keep_ref, table_ref, held, sems = refs
    else:
        corner_ref, side_ref, keep_ref, held, sems = refs
        table_ref = extra_ref
    base = lax.axis_index("head") * half + offset
    copies = [pltpu.make_async_copy(series_ref.at[base + b], held.at[b], sems.at[b]) for b in range(count)]
    for copy in copies:
        copy.start()
    if first:
        fill_table(extra_ref, table_ref, own_modes, series_length)
    middle = table_ref.shape[0] // 2
    for b in range(count):
        copies[b].wait()
        part = jnp.dot(table_ref[...], held[b], preferred_element_type=f32)
        side_ref[b] = part[middle:middle + middle // 2].astype(bf16)
        corner_ref[b] = part[middle + middle // 2:].astype(bf16)
        keep_ref[b] = part[:middle]


def forward(first, series, extra, count, offset, half, own_modes, series_length, rows):
    _, time_count, width = series.shape
    sends = [in_vmem((count, rows // 4, width), bf16)] * 2
    outs = sends + [in_vmem((count, rows // 2, width), f32)]
    if first:
        outs.append(in_vmem((rows, time_count), bf16))
        extra = in_hbm(extra)
    else:
        extra, = held(extra)
    return pl.pallas_call(
        functools.partial(forward_kernel, first, count, offset, half, own_modes, series_length),
        out_shape=outs,
        in_specs=[whole, pl.BlockSpec(memory_space=pltpu.HBM)],
        out_specs=[whole] * len(outs),
        scratch_shapes=[pltpu.VMEM((count, time_count, width), bf16), pltpu.SemaphoreType.DMA((count,))],
        compiler_params=pltpu.CompilerParams(vmem_limit_bytes=16 * 2**20),
        cost_estimate=small,
        name="forward_first" if first else "forward_second",
    )(extra, in_hbm(series))


def onward_kernel(keep_ref, arrived_ref, out_ref):
    middle = keep_ref.shape[1] // 2
    out_ref[...] = (keep_ref[:, middle:] + arrived_ref[:, -middle:].astype(f32)).astype(bf16)


def onward(keep, arrived, cost=small):
    count, rows, width = keep.shape
    return pl.pallas_call(
        onward_kernel,
        out_shape=in_vmem((count, rows // 2, width), bf16),
        in_specs=[whole] * 2,
        out_specs=whole,
        compiler_params=pltpu.CompilerParams(vmem_limit_bytes=16 * 2**20),
        cost_estimate=cost,
        name="sum_onward",
    )(*held(keep, arrived))


def base_kernel(keep_ref, side_ref, out_ref):
    out_ref[...] = keep_ref[:, :side_ref.shape[1]] + side_ref[...].astype(f32)


def base(keep, side):
    return pl.pallas_call(
        base_kernel,
        out_shape=in_vmem(side.shape, f32),
        in_specs=[whole] * 2,
        out_specs=whole,
        compiler_params=pltpu.CompilerParams(vmem_limit_bytes=16 * 2**20),
        cost_estimate=small,
        name="sum_base",
    )(*held(keep, side))


def total_kernel(block_rows, base_ref, second_ref, own_ref, *far_refs):
    total = base_ref[...] + second_ref[...].astype(f32)
    own_ref[...] = total[:, :block_rows]
    for index, ref in enumerate(far_refs):
        ref[...] = total[:, (index + 1) * block_rows:(index + 2) * block_rows].astype(bf16)


def total_rows(base, second, block_rows):
    count, rows, width = second.shape
    if block_rows % 16:
        total = base + second.astype(f32)
        parts = [total[:, start:start + block_rows] for start in range(0, rows, block_rows)]
        return parts[0], [part.astype(bf16) for part in parts[1:]]
    share = (count, block_rows, width)
    parts = pl.pallas_call(
        functools.partial(total_kernel, block_rows),
        out_shape=[in_vmem(share, f32)] + [in_vmem(share, bf16)] * (rows // block_rows - 1),
        in_specs=[whole] * 2,
        out_specs=[whole] * (rows // block_rows),
        compiler_params=pltpu.CompilerParams(vmem_limit_bytes=16 * 2**20),
        cost_estimate=small,
        name="sum_total",
    )(*held(base, second))
    return parts[0], parts[1:]


mix_arrays = 2


def prepare_kernel(weight_ref, query_ref, out_weight_ref, table_ref, *refs):
    modes, heads, size, width = weight_ref.shape
    negative = lax.broadcasted_iota(jnp.int32, (size, width), 1) < size
    for h in range(heads):
        out_ref = refs[h * mix_arrays // heads]
        start = h % (heads // mix_arrays) * modes * 2 * size
        for m in range(modes):
            weight = weight_ref[m, h]
            turned = pltpu.roll(weight, size, 1)
            out_ref[start:start + size] = weight.astype(bf16)
            out_ref[start + size:start + 2 * size] = jnp.where(negative, -turned, turned).astype(bf16)
            start += 2 * size
    out_ref, back_ref = refs[mix_arrays:]
    start = 0
    for ref in (query_ref, out_weight_ref):
        depth, columns = ref.shape
        for first in range(0, columns, width):
            out_ref[start:start + depth] = ref[:, first:first + width]
            start += depth
    back_ref[...] = table_ref[...].T


def prepare(weight, query, out_weight, table):
    modes, heads, size, width = weight.shape
    mixes = in_vmem((modes * heads // mix_arrays * 2 * size, width), bf16)
    outs = pl.pallas_call(
        prepare_kernel,
        out_shape=[mixes] * mix_arrays + [in_vmem((2 * query.size // width, width), bf16), in_vmem(table.shape[::-1], bf16)],
        in_specs=[whole] * 4,
        out_specs=[whole] * (mix_arrays + 2),
        compiler_params=pltpu.CompilerParams(vmem_limit_bytes=16 * 2**20),
        cost_estimate=small,
        name="prepare_weights",
    )(*held(weight, query, out_weight, table))
    return outs[:-1], outs[-1]


def packed_parts(packed, heads, depth):
    weights = packed[-1][...]
    mixes = []
    for array in packed[:-1]:
        step = array.shape[0] * mix_arrays // heads
        mixes += [array[start:start + step] for start in range(0, array.shape[0], step)]
    columns = [weights[start:start + depth] for start in range(0, weights.shape[0], depth)]
    middle = len(columns) // 2
    return mixes, jnp.concatenate(columns[:middle], axis=1), jnp.concatenate(columns[middle:], axis=1)


def split_rows(value):
    high = value.astype(bf16)
    low = (value - high.astype(f32)).astype(bf16)
    return jnp.concatenate([high, low], axis=0)


def fold_rows(value):
    half = value.shape[0] // 2
    return value[:half] + value[half:]


def mix_kernel(scale, own_modes, arrivals, own_ref, *refs):
    arrived = refs[:arrivals]
    packed_refs, (here_ref, there_ref) = refs[arrivals:-2], refs[-2:]
    each = len(packed_refs) // 2
    total = own_ref[...]
    for ref in arrived:
        total = total + ref[...].astype(f32)
    total = total * scale
    count, _, width = total.shape
    rows = count * own_modes
    half = width // 2
    core = lax.axis_index("head")
    pieces = split_rows(jnp.concatenate(
        [total[:, :own_modes].reshape(rows, width), total[:, own_modes:].reshape(rows, width)], axis=0
    ))
    lower = lax.broadcasted_iota(jnp.int32, (rows, 128), 1) < 64
    row_mode = lax.broadcasted_iota(jnp.int32, (2 * rows, 128), 0) & (own_modes - 1)
    mixed, out_weights = [], []
    for packed in (packed_refs[:each], packed_refs[each:]):
        mixes, query, out_weight = packed_parts(packed, half // 64, width)
        out_weights.append(out_weight)
        queries = fold_rows(jnp.dot(pieces, query, preferred_element_type=f32))
        mixed_real, mixed_imag = [], []
        for pair in range(half // 128):
            columns = slice(pair * 128, pair * 128 + 128)
            real, imag = queries[:rows, columns], queries[rows:, columns]
            both = [
                jnp.where(lower, real, pltpu.roll(imag, 64, 1)),
                jnp.where(lower, pltpu.roll(real, 64, 1), imag),
            ]
            heads = []
            for which in range(2):
                spread = split_rows(both[which])
                zero = jnp.zeros_like(spread)
                spread = jnp.concatenate([jnp.where(row_mode == k, spread, zero) for k in range(own_modes)], axis=1)
                heads.append(fold_rows(jnp.dot(spread, mixes[2 * pair + which], preferred_element_type=f32)))
            mixed_real.append(jnp.where(lower, heads[0], pltpu.roll(heads[1], 64, 1)))
            mixed_imag.append(jnp.where(lower, pltpu.roll(heads[0], 64, 1), heads[1]))
        both = jnp.concatenate([jnp.concatenate(mixed_real, axis=1), jnp.concatenate(mixed_imag, axis=1)], axis=0)
        mixed.append(split_rows(both))
    first = jnp.where(core == 0, mixed[0], mixed[1])
    second = jnp.where(core == 0, mixed[1], mixed[0])
    both = jnp.concatenate([first, second], axis=1)
    for out_weight, out_ref in zip(out_weights, (here_ref, there_ref)):
        result = fold_rows(jnp.dot(both, out_weight, preferred_element_type=f32)).astype(bf16)
        out_ref[...] = jnp.concatenate(
            [result[:rows].reshape(count, own_modes, half), result[rows:].reshape(count, own_modes, half)], axis=1
        )


def mix(own, arrived, packed, scale, own_modes):
    count, block_rows, width = own.shape
    here = width // 2
    if own_modes % 8 == 0:
        shape = in_vmem((count, block_rows, here), bf16)
        return pl.pallas_call(
            functools.partial(mix_kernel, scale, own_modes, len(arrived)),
            out_shape=[shape, shape],
            in_specs=[whole] * (1 + len(arrived) + 2 * len(packed[0])),
            out_specs=[whole, whole],
            compiler_params=pltpu.CompilerParams(vmem_limit_bytes=16 * 2**20),
            cost_estimate=small,
            name="mix_modes",
        )(*held(own, *arrived, *packed[0], *packed[1]))
    core = lax.axis_index("head")
    highest = lax.Precision.HIGHEST
    total = (own + sum(piece.astype(f32) for piece in arrived)) * scale
    heads = here // 64
    mixed, results = [], []
    for side in packed:
        mixes, query, _ = packed_parts(side, heads, width)
        projected = jnp.einsum("brf,fg->brg", total, query.astype(f32), precision=highest)
        projected = projected.reshape(count, 2, own_modes, heads, 64)
        weights = jnp.stack(mixes).reshape(heads, own_modes, 2, 64, 2, 64).astype(f32)
        part = jnp.einsum("brmhi,hmriso->bsmho", projected, weights, precision=highest)
        mixed.append(part.reshape(count, block_rows, here))
    mixed = jnp.concatenate(mixed, axis=2)
    mixed = jnp.where(core == 0, mixed, jnp.roll(mixed, here, axis=2))
    for side in packed:
        out_weight = packed_parts(side, heads, width)[2].astype(f32)
        results.append(jnp.einsum("brf,fg->brg", mixed, out_weight, precision=highest).astype(bf16))
    return results


def inverse_kernel(half, offset, start, own, table_ref, *refs):
    pieces, (out_ref, held, sems) = refs[:4], refs[-3:]
    core = lax.axis_index("head")
    copies = []
    for index in range(held.shape[0]):
        b = start + index
        spectra = jnp.concatenate([piece[b] for piece in pieces[:3]] + [pieces[3][index]], axis=0)
        held[index] = jnp.dot(table_ref[...], spectra, preferred_element_type=f32).astype(bf16)
        place = (core ^ (b // own)) * half + offset + b % own
        copies.append(pltpu.make_async_copy(held.at[index], out_ref.at[place], sems.at[index]))
        copies[-1].start()
    for copy in copies:
        copy.wait()


def inverse(table, pieces, previous, series_count, half, offset, start=0):
    time_count, rows = table.shape
    count, _, width = pieces[3].shape
    in_specs = [whole] * 5
    args = held(table, *pieces)
    aliases = {}
    if previous is not None:
        in_specs.append(pl.BlockSpec(memory_space=pltpu.HBM))
        aliases = {len(args): 0}
        args.append(in_hbm(previous))
    return pl.pallas_call(
        functools.partial(inverse_kernel, half, offset, start, pieces[0].shape[0] // 2),
        out_shape=pltpu.HBM((series_count, time_count, width), bf16),
        in_specs=in_specs,
        out_specs=pl.BlockSpec(memory_space=pltpu.HBM),
        scratch_shapes=[pltpu.VMEM((count, time_count, width), bf16), pltpu.SemaphoreType.DMA((count,))],
        input_output_aliases=aliases,
        compiler_params=pltpu.CompilerParams(vmem_limit_bytes=16 * 2**20),
        cost_estimate=small,
        name="inverse_first" if previous is None else "inverse_next",
    )(*args)


def to_devices(value, masks, size):
    pairs = [(2 * i + c, 2 * (i ^ masks[c]) + c) for i in range(size) for c in range(2)]
    return lax.ppermute(value, ("tm", "head"), pairs)


going_first, going_second = (1, 2), (2, 1)


def to_core(value):
    return lax.ppermute(value, "head", [(0, 1), (1, 0)])


def send_far(parts, size):
    return [to_devices(parts[z - 1], (4 * z, 4 * z), size) for z in range(len(parts), 0, -1)]


def join_kernel(*refs):
    out_ref = refs[-1]
    rows = refs[0].shape[1]
    for index, ref in enumerate(refs[:-1]):
        out_ref[:, index * rows:(index + 1) * rows] = ref[...]


def gather_far(block, size):
    far = [to_devices(block, (4 * z, 4 * z), size) for z in range(size // 4 - 1, 0, -1)]
    pieces = [block] + far[::-1]
    count, rows, width = block.shape
    if rows % 16:
        return jnp.concatenate(pieces, axis=1)
    return pl.pallas_call(
        join_kernel,
        out_shape=in_vmem((count, rows * len(pieces), width), bf16),
        in_specs=[whole] * len(pieces),
        out_specs=whole,
        compiler_params=pltpu.CompilerParams(vmem_limit_bytes=16 * 2**20),
        cost_estimate=small,
        name="join_rows",
    )(*held(*pieces))


def body(series, modes, query_weight, mix_weight, out_weight):
    series_count, shard_rows, width = series.shape
    own_modes, heads_here, head_size, _ = mix_weight.shape
    mode_total = modes.shape[0]
    size = lax.axis_size("tm")
    series_length = size * shard_rows
    rows = 2 * mode_total
    half = series_count // 2
    count_a = half // 2
    count_b = half - count_a

    corner_a, side_a, keep_a, table = forward(
        True, series, modes[None, :], count_a, 0, half, own_modes, series_length, rows
    )
    corner_b, side_b, keep_b = forward(False, series, table, count_b, count_a, half, own_modes, series_length, rows)
    block_rows = 2 * own_modes
    scale = 1.0 / math.sqrt(series_length * mode_total)
    corner_a = to_devices(corner_a, going_first, size)
    side_a = to_devices(side_a, going_first, size)
    corner_b = to_devices(corner_b, going_first, size)

    packed, table_back = prepare(mix_weight, query_weight, out_weight, after(table, keep_b))
    packed = [packed, [to_core(array) for array in packed]]

    onward_a = onward(after(keep_a, keep_b, *packed[0]), corner_a)
    second_a = to_devices(onward_a, going_second, size)
    base_a = base(after(keep_a, onward_a), side_a)
    onward_b = onward(after(keep_b, base_a), corner_b, ahead)
    second_b = to_devices(onward_b, going_second, size)
    side_b = to_devices(after(side_b, onward_b), going_first, size)
    own_a, far_a = total_rows(after(base_a, onward_b, *packed[1]), second_a, block_rows)
    far_a = send_far(far_a, size)
    base_b = base(after(keep_b, own_a), side_b)
    own_b, far_b = total_rows(base_b, second_b, block_rows)
    far_b = send_far(far_b, size)

    here_a, there_a = mix(after(own_a, own_b), far_a, packed, scale, own_modes)
    block_a = jnp.concatenate([here_a, to_core(there_a)], axis=0)
    here_b, there_b = mix(after(own_b, block_a), far_b, packed, scale, own_modes)
    block_b = jnp.concatenate([here_b, to_core(there_b)], axis=0)
    rows_a = after(gather_far(block_a, size), block_b)
    second_a = to_devices(rows_a, going_second, size)
    first_a = to_devices(rows_a, going_first, size)
    both_a = to_devices(second_a, going_first, size)
    rows_b = gather_far(block_b, size)
    second_b = to_devices(rows_b, going_second, size)
    first_b = to_devices(rows_b, going_first, size)
    pieces_a = [after(rows_a, second_b), second_a, first_a, both_a]
    output = inverse(table_back, pieces_a, None, series_count, half, 0)
    second_now = after(second_b, first_a)
    both_b = [to_devices(second_now[:count_b], going_first, size), to_devices(second_now[count_b:], going_first, size)]
    for part, start in zip(both_b, (0, count_b)):
        pieces_b = [rows_b, second_b, first_b, part]
        output = inverse(table_back, pieces_b, output, series_count, half, count_a, start)
    return output


def solution(mesh):
    in_specs = (
        P(None, "tm", None),
        P(),
        P(None, "head"),
        P("tm", "head", None, None),
        P(None, "head"),
    )
    out_specs = P(None, "tm", "head")
    return jax.shard_map(body, mesh=mesh, in_specs=in_specs, out_specs=out_specs, check_vma=False)
```

```python
import functools
import math

import jax
import jax.numpy as jnp
from jax import lax
from jax.experimental import pallas as pl
from jax.experimental.pallas import tpu as pltpu
from jax.sharding import PartitionSpec as P

f32 = jnp.float32
bf16 = jnp.bfloat16
two_pi = 2.0 * math.pi


ahead = pl.CostEstimate(flops=3 * 10**9, bytes_accessed=1000, transcendentals=0)


def in_vmem(shape, dtype):
    return pltpu.VMEM(shape, dtype)


def held(*arrays):
    return [pltpu.with_memory_space_constraint(array, pltpu.VMEM) for array in arrays]


def in_hbm(array):
    return pltpu.with_memory_space_constraint(array, pltpu.HBM)


def after(array, *others):
    return lax.optimization_barrier((array, *others))[0]


whole = pl.BlockSpec(memory_space=pltpu.VMEM)
small = pl.CostEstimate(flops=1000, bytes_accessed=1000, transcendentals=0)


def row_modes(place, core, modes_row, rows, own_modes, series_length):
    lanes = modes_row.shape[1]
    row = lax.broadcasted_iota(jnp.int32, (rows, lanes), 0)
    lane = lax.broadcasted_iota(jnp.int32, (rows, lanes), 1)
    far = rows // own_modes // 8
    mode_bits, far_bits = own_modes.bit_length() - 1, far.bit_length() - 1
    block = row >> (mode_bits + 1)
    quarter = block >> far_bits
    relative = ((quarter >> 1) << core) + ((quarter & 1) << (1 - core)) + 4 * (block & (far - 1))
    imaginary = (row >> mode_bits) & 1
    wanted = ((place ^ relative) << mode_bits) + (row & (own_modes - 1))
    picked = jnp.where(lane == wanted, modes_row.astype(f32), 0.0)
    mode = jnp.sum(picked, axis=1, keepdims=True).astype(jnp.int32)
    return mode, imaginary[:, :1] * (series_length // 4)


def wave(phases, series_length):
    turns = phases.astype(f32) * (1.0 / series_length)
    quarters = jnp.floor(turns * 4.0 + 0.5)
    angle = (turns - quarters * 0.25) * two_pi
    square = angle * angle
    cosine = 1.0 + square * (-0.5 + square * (1 / 24 + square * (-1 / 720 + square * (1 / 40320))))
    sine = angle * (1.0 + square * (-1 / 6 + square * (1 / 120 + square * (-1 / 5040))))
    which = quarters.astype(jnp.int32)
    odd = which & 1 == 1
    cos_size = jnp.where(odd, sine, cosine)
    sin_size = jnp.where(odd, cosine, sine)
    cos_flip = (which == 1) | (which == 2)
    sin_flip = (which == 2) | (which == 3)
    return jnp.where(cos_flip, -cos_size, cos_size), jnp.where(sin_flip, -sin_size, sin_size)


def fill_table(modes_ref, table_ref, own_modes, series_length):
    rows, time_count = table_ref.shape
    place = lax.axis_index("tm")
    mode, shift = row_modes(place, lax.axis_index("head"), modes_ref[...], rows, own_modes, series_length)
    lane = lax.broadcasted_iota(jnp.int32, (rows, 128), 1)
    last = series_length - 1
    cos_a, sin_a = wave((mode * (place * time_count + lane * 128) + shift) & last, series_length)
    cos_b, sin_b = wave((mode * lane) & last, series_length)
    for piece in range(time_count // 128):
        value = cos_a[:, piece:piece + 1] * cos_b - sin_a[:, piece:piece + 1] * sin_b
        table_ref[:, piece * 128:piece * 128 + 128] = value.astype(bf16)


def forward_kernel(first, count, offset, half, own_modes, series_length, extra_ref, series_ref, *refs):
    if first:
        corner_ref, side_ref, keep_ref, table_ref, held, sems = refs
    else:
        corner_ref, side_ref, keep_ref, held, sems = refs
        table_ref = extra_ref
    base = lax.axis_index("head") * half + offset
    copies = [pltpu.make_async_copy(series_ref.at[base + b], held.at[b], sems.at[b]) for b in range(count)]
    for copy in copies:
        copy.start()
    if first:
        fill_table(extra_ref, table_ref, own_modes, series_length)
    middle = table_ref.shape[0] // 2
    for b in range(count):
        copies[b].wait()
        part = jnp.dot(table_ref[...], held[b], preferred_element_type=f32)
        side_ref[b] = part[middle:middle + middle // 2].astype(bf16)
        corner_ref[b] = part[middle + middle // 2:].astype(bf16)
        keep_ref[b] = part[:middle]


def forward(first, series, extra, count, offset, half, own_modes, series_length, rows):
    _, time_count, width = series.shape
    sends = [in_vmem((count, rows // 4, width), bf16)] * 2
    outs = sends + [in_vmem((count, rows // 2, width), f32)]
    if first:
        outs.append(in_vmem((rows, time_count), bf16))
        extra = in_hbm(extra)
    else:
        extra, = held(extra)
    return pl.pallas_call(
        functools.partial(forward_kernel, first, count, offset, half, own_modes, series_length),
        out_shape=outs,
        in_specs=[whole, pl.BlockSpec(memory_space=pltpu.HBM)],
        out_specs=[whole] * len(outs),
        scratch_shapes=[pltpu.VMEM((count, time_count, width), bf16), pltpu.SemaphoreType.DMA((count,))],
        compiler_params=pltpu.CompilerParams(vmem_limit_bytes=16 * 2**20),
        cost_estimate=small,
        name="forward_first" if first else "forward_second",
    )(extra, in_hbm(series))


def onward_kernel(keep_ref, arrived_ref, out_ref):
    middle = keep_ref.shape[1] // 2
    out_ref[...] = (keep_ref[:, middle:] + arrived_ref[:, -middle:].astype(f32)).astype(bf16)


def onward(keep, arrived, cost=small):
    count, rows, width = keep.shape
    return pl.pallas_call(
        onward_kernel,
        out_shape=in_vmem((count, rows // 2, width), bf16),
        in_specs=[whole] * 2,
        out_specs=whole,
        compiler_params=pltpu.CompilerParams(vmem_limit_bytes=16 * 2**20),
        cost_estimate=cost,
        name="sum_onward",
    )(*held(keep, arrived))


def base_kernel(keep_ref, side_ref, out_ref):
    out_ref[...] = keep_ref[:, :side_ref.shape[1]] + side_ref[...].astype(f32)


def base(keep, side):
    return pl.pallas_call(
        base_kernel,
        out_shape=in_vmem(side.shape, f32),
        in_specs=[whole] * 2,
        out_specs=whole,
        compiler_params=pltpu.CompilerParams(vmem_limit_bytes=16 * 2**20),
        cost_estimate=small,
        name="sum_base",
    )(*held(keep, side))


def total_kernel(block_rows, base_ref, second_ref, own_ref, *far_refs):
    total = base_ref[...] + second_ref[...].astype(f32)
    own_ref[...] = total[:, :block_rows]
    for index, ref in enumerate(far_refs):
        ref[...] = total[:, (index + 1) * block_rows:(index + 2) * block_rows].astype(bf16)


def total_rows(base, second, block_rows):
    count, rows, width = second.shape
    if block_rows % 16:
        total = base + second.astype(f32)
        parts = [total[:, start:start + block_rows] for start in range(0, rows, block_rows)]
        return parts[0], [part.astype(bf16) for part in parts[1:]]
    share = (count, block_rows, width)
    parts = pl.pallas_call(
        functools.partial(total_kernel, block_rows),
        out_shape=[in_vmem(share, f32)] + [in_vmem(share, bf16)] * (rows // block_rows - 1),
        in_specs=[whole] * 2,
        out_specs=[whole] * (rows // block_rows),
        compiler_params=pltpu.CompilerParams(vmem_limit_bytes=16 * 2**20),
        cost_estimate=small,
        name="sum_total",
    )(*held(base, second))
    return parts[0], parts[1:]


mix_arrays = 2


def prepare_kernel(weight_ref, query_ref, out_weight_ref, table_ref, *refs):
    modes, heads, size, width = weight_ref.shape
    negative = lax.broadcasted_iota(jnp.int32, (size, width), 1) < size
    for h in range(heads):
        out_ref = refs[h * mix_arrays // heads]
        start = h % (heads // mix_arrays) * modes * 2 * size
        for m in range(modes):
            weight = weight_ref[m, h]
            turned = pltpu.roll(weight, size, 1)
            out_ref[start:start + size] = weight.astype(bf16)
            out_ref[start + size:start + 2 * size] = jnp.where(negative, -turned, turned).astype(bf16)
            start += 2 * size
    out_ref, back_ref = refs[mix_arrays:]
    start = 0
    for ref in (query_ref, out_weight_ref):
        depth, columns = ref.shape
        for first in range(0, columns, width):
            out_ref[start:start + depth] = ref[:, first:first + width]
            start += depth
    back_ref[...] = table_ref[...].T


def prepare(weight, query, out_weight, table):
    modes, heads, size, width = weight.shape
    mixes = in_vmem((modes * heads // mix_arrays * 2 * size, width), bf16)
    outs = pl.pallas_call(
        prepare_kernel,
        out_shape=[mixes] * mix_arrays + [in_vmem((2 * query.size // width, width), bf16), in_vmem(table.shape[::-1], bf16)],
        in_specs=[whole] * 4,
        out_specs=[whole] * (mix_arrays + 2),
        compiler_params=pltpu.CompilerParams(vmem_limit_bytes=16 * 2**20),
        cost_estimate=small,
        name="prepare_weights",
    )(*held(weight, query, out_weight, table))
    return outs[:-1], outs[-1]


def packed_parts(packed, heads, depth):
    weights = packed[-1][...]
    mixes = []
    for array in packed[:-1]:
        step = array.shape[0] * mix_arrays // heads
        mixes += [array[start:start + step] for start in range(0, array.shape[0], step)]
    columns = [weights[start:start + depth] for start in range(0, weights.shape[0], depth)]
    middle = len(columns) // 2
    return mixes, jnp.concatenate(columns[:middle], axis=1), jnp.concatenate(columns[middle:], axis=1)


def split_rows(value):
    high = value.astype(bf16)
    low = (value - high.astype(f32)).astype(bf16)
    return jnp.concatenate([high, low], axis=0)


def fold_rows(value):
    half = value.shape[0] // 2
    return value[:half] + value[half:]


def mix_kernel(scale, own_modes, arrivals, own_ref, *refs):
    arrived = refs[:arrivals]
    packed_refs, (here_ref, there_ref) = refs[arrivals:-2], refs[-2:]
    each = len(packed_refs) // 2
    total = own_ref[...]
    for ref in arrived:
        total = total + ref[...].astype(f32)
    total = total * scale
    count, _, width = total.shape
    rows = count * own_modes
    half = width // 2
    core = lax.axis_index("head")
    pieces = split_rows(jnp.concatenate(
        [total[:, :own_modes].reshape(rows, width), total[:, own_modes:].reshape(rows, width)], axis=0
    ))
    lower = lax.broadcasted_iota(jnp.int32, (rows, 128), 1) < 64
    row_mode = lax.broadcasted_iota(jnp.int32, (rows, 128), 0) & (own_modes - 1)
    mixed, out_weights = [], []
    for packed in (packed_refs[:each], packed_refs[each:]):
        mixes, query, out_weight = packed_parts(packed, half // 64, width)
        out_weights.append(out_weight)
        queries = fold_rows(jnp.dot(pieces, query, preferred_element_type=f32))
        mixed_real, mixed_imag = [], []
        for pair in range(half // 128):
            columns = slice(pair * 128, pair * 128 + 128)
            real, imag = queries[:rows, columns], queries[rows:, columns]
            both = [
                jnp.where(lower, real, pltpu.roll(imag, 64, 1)),
                jnp.where(lower, pltpu.roll(real, 64, 1), imag),
            ]
            heads = []
            for which in range(2):
                spread = both[which].astype(bf16)
                zero = jnp.zeros_like(spread)
                spread = jnp.concatenate([jnp.where(row_mode == k, spread, zero) for k in range(own_modes)], axis=1)
                heads.append(jnp.dot(spread, mixes[2 * pair + which], preferred_element_type=f32))
            mixed_real.append(jnp.where(lower, heads[0], pltpu.roll(heads[1], 64, 1)))
            mixed_imag.append(jnp.where(lower, pltpu.roll(heads[0], 64, 1), heads[1]))
        both = jnp.concatenate([jnp.concatenate(mixed_real, axis=1), jnp.concatenate(mixed_imag, axis=1)], axis=0)
        mixed.append(both.astype(bf16))
    first = jnp.where(core == 0, mixed[0], mixed[1])
    second = jnp.where(core == 0, mixed[1], mixed[0])
    both = jnp.concatenate([first, second], axis=1)
    for out_weight, out_ref in zip(out_weights, (here_ref, there_ref)):
        result = jnp.dot(both, out_weight, preferred_element_type=f32).astype(bf16)
        out_ref[...] = jnp.concatenate(
            [result[:rows].reshape(count, own_modes, half), result[rows:].reshape(count, own_modes, half)], axis=1
        )


def mix(own, arrived, packed, scale, own_modes):
    count, block_rows, width = own.shape
    here = width // 2
    if own_modes % 8 == 0:
        shape = in_vmem((count, block_rows, here), bf16)
        return pl.pallas_call(
            functools.partial(mix_kernel, scale, own_modes, len(arrived)),
            out_shape=[shape, shape],
            in_specs=[whole] * (1 + len(arrived) + 2 * len(packed[0])),
            out_specs=[whole, whole],
            compiler_params=pltpu.CompilerParams(vmem_limit_bytes=16 * 2**20),
            cost_estimate=small,
            name="mix_modes",
        )(*held(own, *arrived, *packed[0], *packed[1]))
    core = lax.axis_index("head")
    highest = lax.Precision.HIGHEST
    total = (own + sum(piece.astype(f32) for piece in arrived)) * scale
    heads = here // 64
    mixed, results = [], []
    for side in packed:
        mixes, query, _ = packed_parts(side, heads, width)
        projected = jnp.einsum("brf,fg->brg", total, query.astype(f32), precision=highest)
        projected = projected.reshape(count, 2, own_modes, heads, 64)
        weights = jnp.stack(mixes).reshape(heads, own_modes, 2, 64, 2, 64).astype(f32)
        part = jnp.einsum("brmhi,hmriso->bsmho", projected, weights, precision=highest)
        mixed.append(part.reshape(count, block_rows, here))
    mixed = jnp.concatenate(mixed, axis=2)
    mixed = jnp.where(core == 0, mixed, jnp.roll(mixed, here, axis=2))
    for side in packed:
        out_weight = packed_parts(side, heads, width)[2].astype(f32)
        results.append(jnp.einsum("brf,fg->brg", mixed, out_weight, precision=highest).astype(bf16))
    return results


def inverse_kernel(half, offset, start, own, table_ref, *refs):
    pieces, (out_ref, held, sems) = refs[:4], refs[-3:]
    core = lax.axis_index("head")
    copies = []
    for index in range(held.shape[0]):
        b = start + index
        spectra = jnp.concatenate([piece[b] for piece in pieces[:3]] + [pieces[3][index]], axis=0)
        held[index] = jnp.dot(table_ref[...], spectra, preferred_element_type=f32).astype(bf16)
        place = (core ^ (b // own)) * half + offset + b % own
        copies.append(pltpu.make_async_copy(held.at[index], out_ref.at[place], sems.at[index]))
        copies[-1].start()
    for copy in copies:
        copy.wait()


def inverse(table, pieces, previous, series_count, half, offset, start=0):
    time_count, rows = table.shape
    count, _, width = pieces[3].shape
    in_specs = [whole] * 5
    args = held(table, *pieces)
    aliases = {}
    if previous is not None:
        in_specs.append(pl.BlockSpec(memory_space=pltpu.HBM))
        aliases = {len(args): 0}
        args.append(in_hbm(previous))
    return pl.pallas_call(
        functools.partial(inverse_kernel, half, offset, start, pieces[0].shape[0] // 2),
        out_shape=pltpu.HBM((series_count, time_count, width), bf16),
        in_specs=in_specs,
        out_specs=pl.BlockSpec(memory_space=pltpu.HBM),
        scratch_shapes=[pltpu.VMEM((count, time_count, width), bf16), pltpu.SemaphoreType.DMA((count,))],
        input_output_aliases=aliases,
        compiler_params=pltpu.CompilerParams(vmem_limit_bytes=16 * 2**20),
        cost_estimate=small,
        name="inverse_first" if previous is None else "inverse_next",
    )(*args)


def to_devices(value, masks, size):
    pairs = [(2 * i + c, 2 * (i ^ masks[c]) + c) for i in range(size) for c in range(2)]
    return lax.ppermute(value, ("tm", "head"), pairs)


going_first, going_second = (1, 2), (2, 1)


def to_core(value):
    return lax.ppermute(value, "head", [(0, 1), (1, 0)])


def send_far(parts, size):
    return [to_devices(parts[z - 1], (4 * z, 4 * z), size) for z in range(len(parts), 0, -1)]


def join_kernel(*refs):
    out_ref = refs[-1]
    rows = refs[0].shape[1]
    for index, ref in enumerate(refs[:-1]):
        out_ref[:, index * rows:(index + 1) * rows] = ref[...]


def gather_far(block, size):
    far = [to_devices(block, (4 * z, 4 * z), size) for z in range(size // 4 - 1, 0, -1)]
    pieces = [block] + far[::-1]
    count, rows, width = block.shape
    if rows % 16:
        return jnp.concatenate(pieces, axis=1)
    return pl.pallas_call(
        join_kernel,
        out_shape=in_vmem((count, rows * len(pieces), width), bf16),
        in_specs=[whole] * len(pieces),
        out_specs=whole,
        compiler_params=pltpu.CompilerParams(vmem_limit_bytes=16 * 2**20),
        cost_estimate=small,
        name="join_rows",
    )(*held(*pieces))


def body(series, modes, query_weight, mix_weight, out_weight):
    series_count, shard_rows, width = series.shape
    own_modes, heads_here, head_size, _ = mix_weight.shape
    mode_total = modes.shape[0]
    size = lax.axis_size("tm")
    series_length = size * shard_rows
    rows = 2 * mode_total
    half = series_count // 2
    count_a = half // 2
    count_b = half - count_a

    corner_a, side_a, keep_a, table = forward(
        True, series, modes[None, :], count_a, 0, half, own_modes, series_length, rows
    )
    corner_b, side_b, keep_b = forward(False, series, table, count_b, count_a, half, own_modes, series_length, rows)
    block_rows = 2 * own_modes
    scale = 1.0 / math.sqrt(series_length * mode_total)
    corner_a = to_devices(corner_a, going_first, size)
    side_a = to_devices(side_a, going_first, size)
    corner_b = to_devices(corner_b, going_first, size)

    packed, table_back = prepare(mix_weight, query_weight, out_weight, after(table, keep_b))
    packed = [packed, [to_core(array) for array in packed]]

    onward_a = onward(after(keep_a, keep_b, *packed[0]), corner_a)
    second_a = to_devices(onward_a, going_second, size)
    base_a = base(after(keep_a, onward_a), side_a)
    onward_b = onward(after(keep_b, base_a), corner_b, ahead)
    second_b = to_devices(onward_b, going_second, size)
    side_b = to_devices(after(side_b, onward_b), going_first, size)
    own_a, far_a = total_rows(after(base_a, onward_b, *packed[1]), second_a, block_rows)
    far_a = send_far(far_a, size)
    base_b = base(after(keep_b, own_a), side_b)
    own_b, far_b = total_rows(base_b, second_b, block_rows)
    far_b = send_far(far_b, size)

    here_a, there_a = mix(after(own_a, own_b), far_a, packed, scale, own_modes)
    block_a = jnp.concatenate([here_a, to_core(there_a)], axis=0)
    here_b, there_b = mix(after(own_b, block_a), far_b, packed, scale, own_modes)
    block_b = jnp.concatenate([here_b, to_core(there_b)], axis=0)
    rows_a = after(gather_far(block_a, size), block_b)
    second_a = to_devices(rows_a, going_second, size)
    first_a = to_devices(rows_a, going_first, size)
    both_a = to_devices(second_a, going_first, size)
    rows_b = gather_far(block_b, size)
    second_b = to_devices(rows_b, going_second, size)
    first_b = to_devices(rows_b, going_first, size)
    pieces_a = [after(rows_a, second_b), second_a, first_a, both_a]
    output = inverse(table_back, pieces_a, None, series_count, half, 0)
    second_now = after(second_b, first_a)
    both_b = [to_devices(second_now[:count_b], going_first, size), to_devices(second_now[count_b:], going_first, size)]
    for part, start in zip(both_b, (0, count_b)):
        pieces_b = [rows_b, second_b, first_b, part]
        output = inverse(table_back, pieces_b, output, series_count, half, count_a, start)
    return output


def solution(mesh):
    in_specs = (
        P(None, "tm", None),
        P(),
        P(None, "head"),
        P("tm", "head", None, None),
        P(None, "head"),
    )
    out_specs = P(None, "tm", "head")
    return jax.shard_map(body, mesh=mesh, in_specs=in_specs, out_specs=out_specs, check_vma=False)
```
